256 devices in a mesh: dp: 4 (over x), expert: 64 (over y, z, core).
Axes of the slice: x: 4, y: 4, z: 8, core: 2. Of those that a mesh axis runs over, the one named last changes fastest.
Arguments:
- tokens: bfloat16 [32768, 2560], P(('dp', 'expert')), may hold values from -6 to 6
- cotangent: bfloat16 [32768, 2560], P(('dp', 'expert')), may hold values from -6 to 6
- expert_ids: int32 [32768, 6], P(('dp', 'expert')), may hold values from 0 to 159, all different within a row; in each aligned block of 128 rows (0 to 127, 128 to 255, ...) at most 8 rows name the same one
- gate_weights: float32 [32768, 6], P(('dp', 'expert')), may hold values from 0.1 to 1
- gate_up: bfloat16 [64, 2, 2560, 256], P('expert', None, 'dp'), may hold values from -0.125 to 0.125
- down_proj: bfloat16 [64, 256, 2560], P('expert', None, 'dp'), may hold values from -0.1875 to 0.1875
- gate_up_first: float32 [64, 2, 2560, 256], P('expert', None, 'dp'), may hold values from -18 to 18
- gate_up_second: float32 [64, 2, 2560, 256], P('expert', None, 'dp'), may hold values from 1 to 100
- down_first: float32 [64, 256, 2560], P('expert', None, 'dp'), may hold values from -18 to 18
- down_second: float32 [64, 256, 2560], P('expert', None, 'dp'), may hold values from 1 to 100
Outputs:
- layer_out: bfloat16 [32768, 2560], P(('dp', 'expert'))
- gate_up_new: bfloat16 [64, 2, 2560, 256], P('expert', None, 'dp')
- down_new: bfloat16 [64, 256, 2560], P('expert', None, 'dp')
- gate_up_first_new: float32 [64, 2, 2560, 256], P('expert', None, 'dp')
- gate_up_second_new: float32 [64, 2, 2560, 256], P('expert', None, 'dp')
- down_first_new: float32 [64, 256, 2560], P('expert', None, 'dp')
- down_second_new: float32 [64, 256, 2560], P('expert', None, 'dp')
The draws below stay inside these ranges and needn't reach their ends.
Inputs may be any that keep to these rules, and one draw needn't show every extreme that they name: `expert_ids`: within the 128 rows of one device no expert is named by more than 8 rows.
All inputs are finite; a program needn't handle non-finite values.
Results may differ from the reference program's by a relative error of at most 0.02.
Values may be sent and summed in bfloat16 or wider, within the bound.
A program may use at most 128 MiB of HBM per device.

```python
import math
import jax
import jax.numpy as jnp
import numpy as np
from jax import lax

D = 2560
FF_WIN = 1024
ROUTED = 160
TOP = 6
SPLIT = 4
TOK_DEV = 128
HID = 256
CAP = 8
EXPERTS_WIN = 16
SHARDS = 64
TOKENS = 32768
N_DP = 4
N_EXPERT = 64


def level_of(rng, shape, cuts, low, high):
    level, own = 1.0, jax.random.fold_in(rng, 6)
    for position, blocks in cuts:
        heights = jnp.exp(jax.random.uniform(jax.random.fold_in(own, position), (blocks,), jnp.float32, low / len(cuts), high / len(cuts)))
        level = level * jnp.repeat(heights, shape[position] // blocks).reshape([-1 if axis == position else 1 for axis in range(len(shape))])
    return level


def deal_out(key, own, number, rows, amount, top, most, skew):
    ranking = jax.random.permutation(key, amount)
    heavy_load, ordinary = portions_of(amount, rows * top, most, skew, True), portions_of(amount, rows * top, most, skew, False)
    places = jnp.arange(amount)

    def named(sizes, rotation):
        used = int((sizes > 0).sum())
        fixed = max(1, used // 4)
        shifted = fixed + (places - fixed + rotation * (used - fixed)) % max(1, amount - fixed)
        return jnp.zeros((amount,), jnp.int32).at[ranking[jnp.where(places < fixed, places, shifted)]].set(jnp.asarray(sizes, jnp.int32))

    sizes = jnp.where(number % 4 == 0, named(heavy_load, number // 4), named(ordinary, number - number // 4 - 1))
    mixed = jax.random.permutation(jax.random.fold_in(own, 3), amount)
    donor, taker = mixed[0:amount // 2 * 2:2], mixed[1:amount // 2 * 2:2]
    slack = jnp.minimum(sizes[donor] - 1, most - sizes[taker]) // 2
    slack = jnp.where((donor == ranking[0]) | (taker == ranking[0]) | (sizes[taker] == 0), 0, jnp.maximum(slack, 0))
    shifted = jax.random.randint(jax.random.fold_in(own, 4), (amount // 2,), 0, 1 << 20) % (slack + 1)
    sizes = sizes.at[donor].add(-shifted).at[taker].add(shifted)
    labels = jnp.searchsorted(jnp.cumsum(sizes), jnp.arange(rows * top), side="right").astype(jnp.int32)
    listing = labels.reshape(top, rows).T
    listing = listing[jax.random.permutation(jax.random.fold_in(own, 1), rows)]
    rotation = jax.random.randint(jax.random.fold_in(own, 2), (rows, 1), 0, top)
    return jnp.take_along_axis(listing, (jnp.arange(top)[None, :] + rotation) % top, axis=1)


def portions_of(number_of, total, reach, lean, full):
    loads = [(1 << 20) // math.isqrt(standing ** lean) + 1 for standing in range(1, number_of + 1)]
    largest = reach if full else min(reach, max(-(-total // number_of), total * loads[0] // sum(loads)))
    least = 1 if total - largest >= number_of - 1 else 0
    counts, spare = [largest] + [least] * (number_of - 1), total - largest - least * (number_of - 1)
    while spare > 0:
        candidates = [i for i in range(1, number_of) if counts[i] < largest] or [i for i in range(1, number_of) if counts[i] < reach]
        pool, left = sum([loads[i] for i in candidates]), spare
        for i in candidates:
            addition = min(reach - counts[i], max(1, left * loads[i] // pool), spare)
            counts[i] = counts[i] + addition
            spare = spare - addition
    return np.array(counts)


def bell_draw(rng, shape, spread, limit, cuts=(), kind=jnp.bfloat16):
    values = spread * jax.random.normal(rng, shape, jnp.float32)
    if cuts:
        values = values * level_of(rng, shape, cuts, -0.22, 0.18)
    return jnp.clip(values, -limit, limit).astype(kind)


def setup_inputs(seed: int = 0) -> dict:
    keys = jax.random.split(jax.random.key(seed), 11)
    tokens = bell_draw(keys[0], (TOKENS, D), 1.0, 6.0, ((0, 256),))
    cotangent = bell_draw(keys[1], (TOKENS, D), 1.0, 6.0, ((0, 256),))
    expert_ids_keys = jax.random.split(jax.random.fold_in(keys[2], 1), TOKENS // TOK_DEV)
    expert_ids_turns = jax.random.permutation(jax.random.fold_in(keys[2], 3), TOKENS // TOK_DEV)
    expert_ids = jax.vmap(lambda own, number: deal_out(jax.random.fold_in(keys[2], 2), own, number, TOK_DEV, ROUTED, TOP, CAP, 2))(expert_ids_keys, expert_ids_turns).reshape((TOKENS, TOP))
    gate_weights = jnp.clip(0.1 + 0.9 * jax.random.uniform(keys[3], (TOKENS, TOP), jnp.float32) ** level_of(keys[3], (TOKENS, TOP), ((0, 256),), -0.2, 0.2), 0.1, 1.0)
    gate_up = bell_draw(keys[4], (SHARDS, 2, D, HID), D ** -0.5, 0.125, ((0, 64), (2, 4)))
    down_proj = bell_draw(keys[5], (SHARDS, HID, D), FF_WIN ** -0.5, 0.1875, ((0, 64), (2, 4)))
    gate_up_first = bell_draw(keys[6], (SHARDS, 2, D, HID), 3.0, 18.0, ((0, 64), (2, 4)), jnp.float32)
    gate_up_second = jnp.clip(jnp.exp(math.log(100.0) - 4.6051702 * jax.random.uniform(keys[7], (SHARDS, 2, D, HID), jnp.float32) ** level_of(keys[7], (SHARDS, 2, D, HID), ((0, 64), (2, 4)), -0.2, 0.2)), 1.0, 100.0)
    down_first = bell_draw(keys[8], (SHARDS, HID, D), 3.0, 18.0, ((0, 64), (2, 4)), jnp.float32)
    down_second = jnp.clip(jnp.exp(math.log(100.0) - 4.6051702 * jax.random.uniform(keys[9], (SHARDS, HID, D), jnp.float32) ** level_of(keys[9], (SHARDS, HID, D), ((0, 64), (2, 4)), -0.2, 0.2)), 1.0, 100.0)
    return {"tokens": tokens, "cotangent": cotangent, "expert_ids": expert_ids, "gate_weights": gate_weights, "gate_up": gate_up, "down_proj": down_proj, "gate_up_first": gate_up_first, "gate_up_second": gate_up_second, "down_first": down_first, "down_second": down_second}


beta_one = 0.9
beta_two = 0.95
learn_rate = 0.001
decay_rate = 0.1
step_count = 10.0
epsilon = 1e-08

def pick_slots(choices, experts):
    listed = jnp.arange(experts, dtype=jnp.int32)
    onehot = (choices[:, :, None] == listed[None, None, :]).astype(jnp.int32)
    before = jnp.cumsum(onehot, axis=1) - onehot
    return lax.optimization_barrier(jnp.sum(before * onehot, axis=2)).astype(jnp.int32)

def adamw_update(weight, gradient, first, second):
    first_new = beta_one * first + (1.0 - beta_one) * gradient
    second_new = beta_two * second + (1.0 - beta_two) * gradient * gradient
    first_hat = first_new / (1.0 - beta_one ** step_count)
    second_hat = second_new / (1.0 - beta_two ** step_count)
    weight_float = weight.astype(jnp.float32)
    updated = weight_float - learn_rate * (first_hat / (jnp.sqrt(second_hat) + epsilon) + decay_rate * weight_float)
    return (updated.astype(jnp.bfloat16), first_new, second_new)

def round_partial(values):
    return lax.optimization_barrier(values.astype(jnp.bfloat16)).astype(jnp.float32)

def expert_shard(inputs, grads_in, pair_weights, down_weights):
    pre_gate = jnp.dot(inputs, pair_weights[0], preferred_element_type=jnp.float32)
    pre_up = jnp.dot(inputs, pair_weights[1], preferred_element_type=jnp.float32)
    sigmoid_gate = jax.nn.sigmoid(pre_gate)
    active = (pre_gate * sigmoid_gate * pre_up).astype(jnp.bfloat16)
    partial_out = jnp.dot(active, down_weights, preferred_element_type=jnp.float32).astype(jnp.bfloat16)
    d_active = jnp.dot(grads_in, down_weights.T, preferred_element_type=jnp.float32)
    d_gate = (d_active * pre_up * sigmoid_gate * (1.0 + pre_gate * (1.0 - sigmoid_gate))).astype(jnp.bfloat16)
    d_up = (d_active * pre_gate * sigmoid_gate).astype(jnp.bfloat16)
    grad_gate = jnp.dot(inputs.T, d_gate, preferred_element_type=jnp.float32)
    grad_up = jnp.dot(inputs.T, d_up, preferred_element_type=jnp.float32)
    grad_down = jnp.dot(active.T, grads_in, preferred_element_type=jnp.float32)
    return (partial_out, round_partial(jnp.stack([grad_gate, grad_up])), round_partial(grad_down))

def reference(tokens, cotangent, expert_ids, gate_weights, gate_up, down_proj, gate_up_first, gate_up_second, down_first, down_second):
    groups = N_DP
    experts = EXPERTS_WIN
    slot_rows = N_EXPERT * CAP
    blocks = TOKENS // TOK_DEV
    slot_index = pick_slots(expert_ids.reshape(blocks, TOK_DEV * TOP), experts).reshape(TOKENS, TOP)
    block_index = jnp.arange(TOKENS, dtype=jnp.int32) // TOK_DEV
    group_index = (block_index // N_EXPERT)[:, None]
    source = (block_index % N_EXPERT)[:, None]
    usable = expert_ids < experts
    buffer_rows = groups * experts * slot_rows
    target = jnp.where(usable, ((group_index * experts + expert_ids) * N_EXPERT + source) * CAP + slot_index, buffer_rows).astype(jnp.int32)
    inputs = jnp.zeros((buffer_rows, D), jnp.bfloat16)
    grads_in = jnp.zeros((buffer_rows, D), jnp.bfloat16)
    cot_float = cotangent.astype(jnp.float32)
    for pick in range(TOP):
        inputs = inputs.at[target[:, pick]].set(tokens, mode='drop')
        scaled = (gate_weights[:, pick:pick + 1] * cot_float).astype(jnp.bfloat16)
        grads_in = grads_in.at[target[:, pick]].set(scaled, mode='drop')
    inputs = jnp.swapaxes(inputs.reshape(groups, experts, slot_rows, D), 0, 1)
    grads_in = jnp.swapaxes(grads_in.reshape(groups, experts, slot_rows, D), 0, 1)
    pair_all = gate_up.reshape(experts, SPLIT, 2, D, HID)
    down_all = down_proj.reshape(experts, SPLIT, HID, D)

    def one_expert(operands):
        expert_inputs, expert_grads, expert_pair, expert_down = operands
        outputs = [jnp.zeros((slot_rows, D), jnp.float32) for group_number in range(groups)]
        pair_grads = []
        down_grads = []
        for part_index in range(SPLIT):
            pair_total = jnp.zeros((2, D, HID), jnp.float32)
            down_total = jnp.zeros((HID, D), jnp.float32)
            for group_number in range(groups):
                partial_out, pair_grad, down_grad = expert_shard(expert_inputs[group_number], expert_grads[group_number], expert_pair[part_index], expert_down[part_index])
                outputs[group_number] = outputs[group_number] + partial_out.astype(jnp.float32)
                pair_total = pair_total + pair_grad
                down_total = down_total + down_grad
            pair_grads.append(pair_total)
            down_grads.append(down_total)
        return (jnp.stack(outputs), jnp.stack(pair_grads), jnp.stack(down_grads))
    combined, pair_grads, down_grads = lax.map(one_expert, (inputs, grads_in, pair_all, down_all))
    combined = jnp.swapaxes(combined, 0, 1).reshape(buffer_rows, D)
    layer_out = jnp.zeros((TOKENS, D), jnp.float32)
    for pick in range(TOP):
        taken = combined[jnp.minimum(target[:, pick], buffer_rows - 1)]
        layer_out = layer_out + jnp.where(usable[:, pick:pick + 1], gate_weights[:, pick:pick + 1], 0.0) * taken
    layer_out = layer_out.astype(jnp.bfloat16)
    pair_grads = pair_grads.reshape(SHARDS, 2, D, HID)
    down_grads = down_grads.reshape(SHARDS, HID, D)
    gate_up_new, gate_up_first_new, gate_up_second_new = adamw_update(gate_up, pair_grads, gate_up_first, gate_up_second)
    down_new, down_first_new, down_second_new = adamw_update(down_proj, down_grads, down_first, down_second)
    return (layer_out, gate_up_new, down_new, gate_up_first_new, gate_up_second_new, down_first_new, down_second_new)
```

```python
import functools

import jax
import jax.numpy as jnp
from jax import lax
from jax.experimental import pallas as pl
from jax.experimental.pallas import tpu as pltpu
from jax.sharding import PartitionSpec as P

TOP = 6
SPLIT = 4
CAP = 8
PAIR = 2 * CAP
NY = 4
MESH = pl.DeviceIdType.MESH

beta_one = 0.9
beta_two = 0.95
learn_rate = 0.001
decay_rate = 0.1
step_count = 10.0
epsilon = 1e-08


def adamw_update(weight, gradient, first, second):
    first_new = beta_one * first + (1.0 - beta_one) * gradient
    second_new = beta_two * second + (1.0 - beta_two) * gradient * gradient
    first_hat = first_new / (1.0 - beta_one**step_count)
    second_hat = second_new / (1.0 - beta_two**step_count)
    weight_float = weight.astype(jnp.float32)
    updated = weight_float - learn_rate * (
        first_hat / (jnp.sqrt(second_hat) + epsilon) + decay_rate * weight_float
    )
    return (updated.astype(jnp.bfloat16), first_new, second_new)


def dot(left, right):
    return jnp.dot(left, right, preferred_element_type=jnp.float32)


def chunk_of(size):
    return 512 if size % 512 == 0 else 128


def moe_kernel(
    ny,
    nz,
    tokens,
    cot,
    ids,
    gates,
    gu_own,
    dn_own,
    out,
    gpair,
    gdown,
    pack,
    comb,
    xy,
    wgu,
    wd,
    gacc,
    gs,
    part_l,
    part_r,
    from_l,
    from_r,
    zbuf,
    zrecv,
    sbuf,
    orecv,
    own_sem,
    wsend,
    wrecv,
    dsend,
    psend,
    ssend,
    near_sem,
    pair_sem,
    sib_sem,
    zsend,
    zwait,
    osend,
    owait,
    rsend,
    rwait,
    self_sem,
):
    nh = nz // 2
    experts = ny * nh
    slots = experts * CAP
    rows_t, feat = tokens.shape
    part = feat // 4
    hid = wd.shape[0]
    half, hhid = part // 2, hid // 2
    lanes = feat // 2
    batch = 4 * ny * PAIR

    g = lax.axis_index("dp")
    ei = lax.axis_index("expert")
    core = lax.rem(ei, 2)
    chip = lax.div(ei, 2)
    z = lax.rem(chip, nz)
    y = lax.div(chip, nz)
    pz = lax.rem(z, 2)
    right, left = (lax.rem(g + 1, 4), ei), (lax.rem(g + 3, 4), ei)
    sib = (g, ei + 1 - 2 * core)
    mate = (g, ei + 2 - 4 * pz)

    def device(yy, zz):
        return (g, (yy * nz + zz) * 2 + core)

    barrier = pltpu.get_barrier_semaphore()

    def greet(step, carry):
        other = lax.rem(chip + step, ny * nz)
        pl.semaphore_signal(
            barrier, inc=1, device_id=(g, other * 2 + core), device_id_type=MESH
        )
        return carry

    for who in (left, right, sib):
        pl.semaphore_signal(barrier, inc=1, device_id=who, device_id_type=MESH)
    lax.fori_loop(1, ny * nz, greet, 0)

    own_copies = [
        pltpu.make_async_copy(
            gu_own, wgu.at[:, pl.ds(pl.multiple_of(g * part, 128), part)], own_sem.at[0]
        ),
        pltpu.make_async_copy(
            dn_own, wd.at[:, pl.ds(pl.multiple_of(g * part, 128), part)], own_sem.at[1]
        ),
    ]
    for copy in own_copies:
        copy.start()

    expert_of = lax.broadcasted_iota(jnp.int32, (rows_t, slots), 1) // CAP
    place_of = lax.broadcasted_iota(jnp.int32, (rows_t, slots), 1) % CAP
    named = jnp.zeros((rows_t, slots), jnp.float32)
    weight = jnp.zeros((rows_t, slots), jnp.float32)
    for k in range(TOP):
        hit = ids[:, k : k + 1] == expert_of
        named = jnp.where(hit, 1.0, named)
        weight = jnp.where(hit, gates[:, k : k + 1], weight)
    earlier = lax.broadcasted_iota(jnp.int32, (rows_t, rows_t), 0) > lax.broadcasted_iota(
        jnp.int32, (rows_t, rows_t), 1
    )
    before = dot(
        jnp.where(earlier, 1.0, 0.0).astype(jnp.bfloat16), named.astype(jnp.bfloat16)
    )
    chosen = jnp.where(before == place_of.astype(jnp.float32), named, 0.0)
    scale = chosen * weight
    high = scale.astype(jnp.bfloat16)
    comb[0] = high
    comb[1] = (scale - high.astype(jnp.float32)).astype(jnp.bfloat16)
    pick = chosen.T.astype(jnp.bfloat16)
    slot_weight = jnp.sum(scale.T, axis=1, keepdims=True)
    kc = chunk_of(feat)
    for at in range(0, feat, kc):
        xs = dot(pick, tokens[:, at : at + kc]).reshape(experts, CAP, kc)
        ys = (dot(pick, cot[:, at : at + kc]) * slot_weight).reshape(experts, CAP, kc)
        both = jnp.concatenate([xs, ys], axis=1).reshape(experts * PAIR, kc)
        pack[:, at : at + kc] = both.astype(jnp.bfloat16)

    pl.semaphore_wait(barrier, ny * nz + 2)

    def weight_parts(owner, hf):
        return (
            wgu.at[:, pl.ds(pl.multiple_of(owner * part + hf * half, 64), half)],
            wd.at[pl.ds(hf * hhid, hhid), pl.ds(pl.multiple_of(owner * part, 128), part)],
        )

    def weight_copy(src_refs, owner, hf, lane, whom):
        return [
            pltpu.make_async_remote_copy(
                src_ref=s,
                dst_ref=d,
                send_sem=wsend.at[lane, hf, i],
                recv_sem=wrecv.at[lane, hf, i],
                device_id=whom,
                device_id_type=MESH,
            )
            for i, (s, d) in enumerate(
                zip(src_refs, weight_parts(owner, hf), strict=True)
            )
        ]

    def own_parts(hf):
        return (
            gu_own.at[:, pl.ds(hf * half, half)],
            dn_own.at[pl.ds(hf * hhid, hhid)],
        )

    g_left, g_right, g_opp = lax.rem(g + 3, 4), lax.rem(g + 1, 4), lax.rem(g + 2, 4)
    weight_sends = []
    for turn in range(2):
        for lane, whom in ((0, right), (1, left)):
            hf = turn if lane == 0 else 1 - turn
            weight_sends += weight_copy(own_parts(hf), g, hf, lane, whom)
    for copy in weight_sends:
        copy.start()

    def slot_rows(h, q, ry, count=1):
        return xy.at[pl.ds(pl.multiple_of(((h * 4 + q) * ny + ry) * PAIR, PAIR), count * PAIR)]

    def near_copy(h, ry):
        sign = 1 - 2 * lax.rem(h + pz, 2)
        zt = lax.rem(z + sign * h + nz, nz)
        yt = lax.rem(y + ry, ny)
        to = yt * nh + lax.div(zt, 2)
        return pltpu.make_async_remote_copy(
            src_ref=pack.at[pl.ds(pl.multiple_of(to * PAIR, PAIR), PAIR)],
            dst_ref=slot_rows(h, 0, ry),
            send_sem=dsend,
            recv_sem=near_sem.at[h * ny + ry],
            device_id=device(yt, zt),
            device_id_type=MESH,
        )

    mine = pltpu.make_async_copy(
        pack.at[pl.ds(pl.multiple_of(lax.div(ei, 4) * PAIR, PAIR), PAIR)],
        slot_rows(0, 0, 0),
        near_sem.at[0],
    )
    mine.start()
    for h in range(nh):
        for ry in range(ny):
            if h or ry:
                near_copy(h, ry).start()

    def hand_on(h, q, ry, whom, to_q, send_sem, recv_sem):
        return pltpu.make_async_remote_copy(
            src_ref=slot_rows(h, q, ry),
            dst_ref=slot_rows(h, to_q, ry),
            send_sem=send_sem,
            recv_sem=recv_sem,
            device_id=whom,
            device_id_type=MESH,
        )

    def arrived(ref, sem):
        pltpu.make_async_copy(ref, ref, sem).wait()

    def pass_near(h, ry):
        arrived(slot_rows(h, 0, ry), near_sem.at[h * ny + ry])
        hand_on(h, 0, ry, mate, 1, psend, pair_sem.at[h * ny + ry]).start()
        hand_on(h, 0, ry, sib, 2, ssend, sib_sem.at[h, 0]).start()

    def pass_pair(h, ry):
        arrived(slot_rows(h, 1, ry), pair_sem.at[h * ny + ry])
        hand_on(h, 1, ry, sib, 3, ssend, sib_sem.at[h, 1]).start()

    def pass_weights(lane, hf, owner, whom):
        for i, ref in enumerate(weight_parts(owner, hf)):
            arrived(ref, wrecv.at[lane, hf, i])
        copies = weight_copy(weight_parts(owner, hf), owner, hf, 2, whom)
        for copy in copies:
            copy.start()
        return copies

    gacc[...] = jnp.zeros_like(gacc)
    for h in range(nh - 1):
        for ry in range(ny):
            pass_near(h, ry)
        for ry in range(ny):
            pass_pair(h, ry)
        if h == 0:
            weight_sends += pass_weights(0, 0, g_left, right)
            weight_sends += pass_weights(1, 1, g_right, left)
    for h in range(nh - 1):
        for q in range(2):
            arrived(slot_rows(h, 2 + q, 0, ny), sib_sem.at[h, q])
    for copy in own_copies:
        copy.wait()
    for lane, hf, owner in (
        (0, 1, g_left),
        (1, 0, g_right),
        (2, 0, g_opp),
        (2, 1, g_opp),
    ):
        for i, ref in enumerate(weight_parts(owner, hf)):
            arrived(ref, wrecv.at[lane, hf, i])

    last = nh - 1

    def z_copy(h):
        return pltpu.make_async_remote_copy(
            src_ref=zbuf.at[pl.ds(pl.multiple_of(h * batch + batch // 2, PAIR), batch // 2)],
            dst_ref=zrecv.at[pl.ds(pl.multiple_of(h * (batch // 2), PAIR), batch // 2)],
            send_sem=zsend.at[h],
            recv_sem=zwait.at[h],
            device_id=sib,
            device_id_type=MESH,
        )

    def step(h, carry):
        @pl.when(h < ny)
        def _():
            pass_near(last, h)
            pass_pair(last, h)

        @pl.when(h == last)
        def _():
            for ry in range(nh, ny):
                pass_near(last, ry)
                pass_pair(last, ry)
            for q in range(2):
                arrived(slot_rows(last, 2 + q, 0, ny), sib_sem.at[last, q])

        rows = pl.ds(pl.multiple_of(h * batch, batch), batch)
        wide = (batch, hid)
        pre = jnp.zeros(wide, jnp.float32)
        up = jnp.zeros(wide, jnp.float32)
        err = jnp.zeros(wide, jnp.float32)
        for at in range(0, feat, kc):
            block = xy[rows, at : at + kc]
            pre += dot(block, wgu[0, at : at + kc])
            up += dot(block, wgu[1, at : at + kc])
            err += lax.dot_general(
                block,
                wd[:, at : at + kc],
                (((1,), (1,)), ((), ())),
                preferred_element_type=jnp.float32,
            )
        pre = pre.reshape(batch // PAIR, PAIR, hid)[:, :CAP]
        up = up.reshape(batch // PAIR, PAIR, hid)[:, :CAP]
        err = err.reshape(batch // PAIR, PAIR, hid)[:, CAP:]
        sig = jax.nn.sigmoid(pre)
        active = pre * sig * up
        d_gate = err * up * sig * (1.0 + pre * (1.0 - sig))
        d_up = err * pre * sig
        none = jnp.zeros_like(active)
        spread = jnp.concatenate(
            [
                jnp.concatenate([d_gate, d_up, none], axis=2),
                jnp.concatenate([none, none, active], axis=2),
            ],
            axis=1,
        )
        spread = spread.reshape(batch, 3 * hid).astype(jnp.bfloat16)
        for at in range(0, feat, part):
            gacc[at : at + part] += lax.dot_general(
                xy[rows, at : at + part],
                spread,
                (((0,), (0,)), ((), ())),
                preferred_element_type=jnp.float32,
            )
        act = active.reshape(batch // 2, hid).astype(jnp.bfloat16)
        kz = chunk_of(lanes) if lanes % 512 == 0 else (256 if lanes % 256 == 0 else 128)
        for at in range(0, lanes, kz):
            low = dot(act, wd[:, at : at + kz])
            top = dot(act, wd[:, lanes + at : lanes + at + kz])
            both = jnp.concatenate(
                [
                    low.reshape(batch // PAIR, CAP, kz),
                    top.reshape(batch // PAIR, CAP, kz),
                ],
                axis=1,
            )
            zbuf[rows, at : at + kz] = both.reshape(batch, kz).astype(jnp.bfloat16)
        z_copy(h).start()
        return carry

    lax.fori_loop(0, nh, step, 0)

    def grad_rows(owner, hf):
        return pl.ds(pl.multiple_of(owner * part + hf * half, 64), half)

    def grad_copy(k, src, dst, whom):
        return pltpu.make_async_remote_copy(
            src_ref=src,
            dst_ref=dst,
            send_sem=rsend.at[k],
            recv_sem=rwait.at[k],
            device_id=whom,
            device_id_type=MESH,
        )

    def gs_half(k, hf):
        return gs.at[k, pl.ds(hf * half, half)]

    def half_of(ref, hf):
        return ref.at[pl.ds(hf * half, half)]

    grad_sends = [
        grad_copy(0, gs_half(0, 0), part_l, right),
        grad_copy(1, gs_half(0, 1), part_r, left),
        grad_copy(2, gs_half(1, 1), half_of(from_l, 1), right),
        grad_copy(3, gs_half(2, 0), half_of(from_r, 0), left),
        grad_copy(4, gs_half(1, 0), half_of(from_l, 0), right),
        grad_copy(5, gs_half(2, 1), half_of(from_r, 1), left),
    ]
    for k, (slot, hf, owner) in enumerate(
        ((0, 0, g_opp), (0, 1, g_opp), (1, 1, g_right), (2, 0, g_left))
    ):
        gs[slot, hf * half : (hf + 1) * half] = gacc[grad_rows(owner, hf)].astype(
            jnp.bfloat16
        )
        grad_sends[k].start()

    def o_copy(h, q, ry):
        ys = lax.rem(y - ry + ny, ny)
        if q == 0:
            zs = lax.rem(z + (2 * pz - 1) * h + nz, nz)
        else:
            zs = lax.rem(z + (1 - 2 * pz) * (1 + h) + nz, nz)
        return pltpu.make_async_remote_copy(
            src_ref=sbuf.at[pl.ds(pl.multiple_of(((h * 2 + q) * ny + ry) * PAIR, PAIR), PAIR)],
            dst_ref=orecv.at[pl.ds(pl.multiple_of((pz * experts + lax.div(ei, 4)) * PAIR, PAIR), PAIR)],
            send_sem=osend,
            recv_sem=owait,
            device_id=device(ys, zs),
            device_id_type=MESH,
        )

    for h in range(nh):
        z_copy(h).wait_recv()
        a, b = h * batch, h * (batch // 2)
        total = zbuf[a : a + batch // 2].astype(jnp.float32) + zrecv[
            b : b + batch // 2
        ].astype(jnp.float32)
        sbuf[b : b + batch // 2] = total.astype(jnp.bfloat16)
        for q in range(2):
            for ry in range(ny):
                if h or q or ry:
                    o_copy(h, q, ry).start()
                else:
                    pltpu.make_async_copy(
                        sbuf.at[pl.ds(0, PAIR)],
                        orecv.at[pl.ds(pl.multiple_of((pz * experts + lax.div(ei, 4)) * PAIR, PAIR), PAIR)],
                        owait,
                    ).start()

    for k, (came, slot, hf, owner) in enumerate(
        ((part_l, 1, 0, g_right), (part_r, 2, 1, g_left))
    ):
        arrived(came, rwait.at[k])
        gs[slot, hf * half : (hf + 1) * half] = (
            gacc[grad_rows(owner, hf)] + came[...].astype(jnp.float32)
        ).astype(jnp.bfloat16)
        grad_sends[4 + k].start()

    arrived(orecv, owait)
    for side in range(2):
        done = jnp.zeros((rows_t, lanes), jnp.float32)
        for which in range(2):
            part_o = orecv[which * experts * PAIR : (which + 1) * experts * PAIR]
            part_o = part_o.astype(jnp.float32).reshape(experts, PAIR, lanes)
            part_o = part_o[:, side * CAP : (side + 1) * CAP].reshape(slots, lanes)
            part_o = part_o.astype(jnp.bfloat16)
            done += dot(comb[0], part_o) + dot(comb[1], part_o)
        out[:, side * lanes : (side + 1) * lanes] = done.astype(jnp.bfloat16)

    for first, second, hf in ((3, 4, 0), (2, 5, 1)):
        for k in (first, second):
            dst = half_of(from_l if k in (2, 4) else from_r, hf)
            arrived(dst, rwait.at[k])
        at = hf * half
        total = (
            gacc[grad_rows(g, hf)]
            + from_l[at : at + half].astype(jnp.float32)
            + from_r[at : at + half].astype(jnp.float32)
        )
        gpair[0, at : at + half] = total[:, :hid]
        gpair[1, at : at + half] = total[:, hid : 2 * hid]
        gdown[at : at + half] = total[:, 2 * hid :]

    for copy in weight_sends + grad_sends:
        copy.wait_send()
    for h in range(nh):
        z_copy(h).wait_send()
    count = nh * ny
    arrived(xy.at[pl.ds(0, (count - 1) * PAIR)], dsend)
    arrived(xy.at[pl.ds(0, count * PAIR)], psend)
    arrived(xy.at[pl.ds(0, 2 * count * PAIR)], ssend)
    arrived(sbuf.at[pl.ds(0, (2 * count - 1) * PAIR)], osend)


def experts_step(tokens, cotangent, expert_ids, gate_weights, pair_own, down_own):
    shards = lax.axis_size("expert")
    ny, nz = NY, shards // (2 * NY)
    nh = nz // 2
    experts = shards // SPLIT
    rows, feat = tokens.shape
    hid = down_own.shape[0]
    part, lanes = feat // 4, feat // 2
    slots = experts * CAP
    batch = 4 * ny * PAIR
    vmem = pl.BlockSpec(memory_space=pltpu.VMEM)
    hbm = pl.BlockSpec(memory_space=pl.ANY)
    bf, f32 = jnp.bfloat16, jnp.float32
    dma = pltpu.SemaphoreType.DMA
    return pl.pallas_call(
        functools.partial(moe_kernel, ny, nz),
        out_shape=(
            jax.ShapeDtypeStruct((rows, feat), bf),
            jax.ShapeDtypeStruct((2, part, hid), f32),
            jax.ShapeDtypeStruct((part, hid), f32),
        ),
        in_specs=[vmem, vmem, vmem, vmem, hbm, hbm],
        out_specs=(vmem, vmem, vmem),
        scratch_shapes=[
            pltpu.VMEM((experts * PAIR, feat), bf),
            pltpu.VMEM((2, rows, slots), bf),
            pltpu.VMEM((nh * batch, feat), bf),
            pltpu.VMEM((2, feat, hid), bf),
            pltpu.VMEM((hid, feat), bf),
            pltpu.VMEM((feat, 3 * hid), f32),
            pltpu.VMEM((3, part, 3 * hid), bf),
            pltpu.VMEM((part // 2, 3 * hid), bf),
            pltpu.VMEM((part // 2, 3 * hid), bf),
            pltpu.VMEM((part, 3 * hid), bf),
            pltpu.VMEM((part, 3 * hid), bf),
            pltpu.VMEM((nh * batch, lanes), bf),
            pltpu.VMEM((nh * batch // 2, lanes), bf),
            pltpu.VMEM((nh * batch // 2, lanes), bf),
            pltpu.VMEM((2 * experts * PAIR, lanes), bf),
            dma((2,)),
            dma((3, 2, 2)),
            dma((3, 2, 2)),
            dma,
            dma,
            dma,
            dma((nh * ny,)),
            dma((nh * ny,)),
            dma((nh, 2)),
            dma((nh,)),
            dma((nh,)),
            dma,
            dma,
            dma((6,)),
            dma((6,)),
            dma,
        ],
        compiler_params=pltpu.CompilerParams(
            collective_id=0,
            has_side_effects=True,
            vmem_limit_bytes=60 * 1024 * 1024,
        ),
        cost_estimate=pl.CostEstimate(
            flops=8_000_000_000, bytes_accessed=10_000_000, transcendentals=200_000
        ),
    )(tokens, cotangent, expert_ids, gate_weights, pair_own, down_own)


def body(
    tokens,
    cotangent,
    expert_ids,
    gate_weights,
    gate_up,
    down_proj,
    gate_up_first,
    gate_up_second,
    down_first,
    down_second,
):
    layer_out, own_pair, own_down = experts_step(
        tokens, cotangent, expert_ids, gate_weights, gate_up[0], down_proj[0]
    )
    gate_up_new, gate_up_first_new, gate_up_second_new = adamw_update(
        gate_up, own_pair[None], gate_up_first, gate_up_second
    )
    down_new, down_first_new, down_second_new = adamw_update(
        down_proj, own_down.T[None], down_first, down_second
    )
    return (
        layer_out,
        gate_up_new,
        down_new,
        gate_up_first_new,
        gate_up_second_new,
        down_first_new,
        down_second_new,
    )


def solution(mesh):
    return jax.shard_map(
        body,
        mesh=mesh,
        in_specs=(
            P(("dp", "expert"), None),
            P(("dp", "expert"), None),
            P(("dp", "expert"), None),
            P(("dp", "expert"), None),
            P("expert", None, "dp", None),
            P("expert", None, "dp"),
            P("expert", None, "dp", None),
            P("expert", None, "dp", None),
            P("expert", None, "dp"),
            P("expert", None, "dp"),
        ),
        out_specs=(
            P(("dp", "expert"), None),
            P("expert", None, "dp", None),
            P("expert", None, "dp"),
            P("expert", None, "dp", None),
            P("expert", None, "dp", None),
            P("expert", None, "dp"),
            P("expert", None, "dp"),
        ),
        check_vma=False,
    )
```

```python
import functools

import jax
import jax.numpy as jnp
from jax import lax
from jax.experimental import pallas as pl
from jax.experimental.pallas import tpu as pltpu
from jax.sharding import PartitionSpec as P

TOP = 6
SPLIT = 4
CAP = 8
PAIR = 2 * CAP
NY = 4
MESH = pl.DeviceIdType.MESH

beta_one = 0.9
beta_two = 0.95
learn_rate = 0.001
decay_rate = 0.1
step_count = 10.0
epsilon = 1e-08


def adamw_update(weight, gradient, first, second):
    first_new = beta_one * first + (1.0 - beta_one) * gradient
    second_new = beta_two * second + (1.0 - beta_two) * gradient * gradient
    first_hat = first_new / (1.0 - beta_one**step_count)
    second_hat = second_new / (1.0 - beta_two**step_count)
    weight_float = weight.astype(jnp.float32)
    updated = weight_float - learn_rate * (
        first_hat / (jnp.sqrt(second_hat) + epsilon) + decay_rate * weight_float
    )
    return (updated.astype(jnp.bfloat16), first_new, second_new)


def dot(left, right):
    return jnp.dot(left, right, preferred_element_type=jnp.float32)


def chunk_of(size):
    return 512 if size % 512 == 0 else 128


def moe_kernel(
    ny,
    nz,
    tokens_in,
    cot_in,
    ids_in,
    gates_in,
    gu_own,
    dn_own,
    out,
    gpair,
    gdown,
    tokens,
    cot,
    ids,
    gates,
    pack,
    comb,
    xy,
    wgu,
    wd,
    gacc,
    gs,
    part_l,
    part_r,
    from_l,
    from_r,
    zbuf,
    zrecv,
    sbuf,
    orecv,
    own_sem,
    wsend,
    wrecv,
    dsend,
    psend,
    ssend,
    near_sem,
    pair_sem,
    sib_sem,
    zsend,
    zwait,
    osend,
    owait,
    rsend,
    rwait,
    in_sem,
):
    nh = nz // 2
    experts = ny * nh
    slots = experts * CAP
    rows_t, feat = tokens.shape
    part = feat // 4
    hid = wd.shape[0]
    half, hhid = part // 2, hid // 2
    lanes = feat // 2
    batch = 4 * ny * PAIR

    g = lax.axis_index("dp")
    ei = lax.axis_index("expert")
    core = lax.rem(ei, 2)
    chip = lax.div(ei, 2)
    z = lax.rem(chip, nz)
    y = lax.div(chip, nz)
    pz = lax.rem(z, 2)
    right, left = (lax.rem(g + 1, 4), ei), (lax.rem(g + 3, 4), ei)
    sib = (g, ei + 1 - 2 * core)
    mate = (g, ei + 2 - 4 * pz)

    def device(yy, zz):
        return (g, (yy * nz + zz) * 2 + core)

    loads = [
        pltpu.make_async_copy(src, dst, in_sem.at[i])
        for i, (src, dst) in enumerate(
            ((ids_in, ids), (gates_in, gates), (tokens_in, tokens), (cot_in, cot))
        )
    ]
    for copy in loads:
        copy.start()

    barrier = pltpu.get_barrier_semaphore()

    def greet(step, carry):
        other = lax.rem(chip + step, ny * nz)
        pl.semaphore_signal(
            barrier, inc=1, device_id=(g, other * 2 + core), device_id_type=MESH
        )
        return carry

    for who in (left, right, sib):
        pl.semaphore_signal(barrier, inc=1, device_id=who, device_id_type=MESH)
    lax.fori_loop(1, ny * nz, greet, 0)

    own_copies = [
        pltpu.make_async_copy(
            gu_own, wgu.at[:, pl.ds(pl.multiple_of(g * part, 128), part)], own_sem.at[0]
        ),
        pltpu.make_async_copy(
            dn_own, wd.at[:, pl.ds(pl.multiple_of(g * part, 128), part)], own_sem.at[1]
        ),
    ]
    for copy in own_copies:
        copy.start()
    for copy in loads:
        copy.wait()

    row = lax.broadcasted_iota(jnp.int32, (slots, rows_t), 0)
    named = jnp.zeros((slots, rows_t), jnp.float32)
    weight = jnp.zeros((slots, rows_t), jnp.float32)
    for k in range(TOP):
        hit = ids[k : k + 1] == row // CAP
        named = jnp.where(hit, 1.0, named)
        weight = jnp.where(hit, gates[k : k + 1], weight)
    earlier = lax.broadcasted_iota(jnp.int32, (rows_t, rows_t), 0) < lax.broadcasted_iota(
        jnp.int32, (rows_t, rows_t), 1
    )
    before = dot(
        named.astype(jnp.bfloat16), jnp.where(earlier, 1.0, 0.0).astype(jnp.bfloat16)
    )
    chosen = jnp.where(before == (row % CAP).astype(jnp.float32), named, 0.0)
    scale = chosen * weight
    pick = chosen.astype(jnp.bfloat16)
    slot_weight = jnp.sum(scale, axis=1, keepdims=True)
    back = scale.T
    high = back.astype(jnp.bfloat16)
    comb[0] = high
    comb[1] = (back - high.astype(jnp.float32)).astype(jnp.bfloat16)
    kc = chunk_of(feat)
    for at in range(0, feat, kc):
        xs = dot(pick, tokens[:, at : at + kc]).reshape(experts, CAP, kc)
        ys = (dot(pick, cot[:, at : at + kc]) * slot_weight).reshape(experts, CAP, kc)
        both = jnp.concatenate([xs, ys], axis=1).reshape(experts * PAIR, kc)
        pack[:, at : at + kc] = both.astype(jnp.bfloat16)

    gacc[...] = jnp.zeros_like(gacc)

    pl.semaphore_wait(barrier, ny * nz + 2)

    def weight_parts(owner, hf):
        return (
            wgu.at[:, pl.ds(pl.multiple_of(owner * part + hf * half, 64), half)],
            wd.at[pl.ds(hf * hhid, hhid), pl.ds(pl.multiple_of(owner * part, 128), part)],
        )

    def weight_copy(src_refs, owner, hf, lane, whom):
        return [
            pltpu.make_async_remote_copy(
                src_ref=s,
                dst_ref=d,
                send_sem=wsend.at[lane, hf, i],
                recv_sem=wrecv.at[lane, hf, i],
                device_id=whom,
                device_id_type=MESH,
            )
            for i, (s, d) in enumerate(
                zip(src_refs, weight_parts(owner, hf), strict=True)
            )
        ]

    def own_parts(hf):
        return (
            gu_own.at[:, pl.ds(hf * half, half)],
            dn_own.at[pl.ds(hf * hhid, hhid)],
        )

    g_left, g_right, g_opp = lax.rem(g + 3, 4), lax.rem(g + 1, 4), lax.rem(g + 2, 4)
    weight_sends = []
    for turn in range(2):
        for lane, whom in ((0, right), (1, left)):
            hf = turn if lane == 0 else 1 - turn
            weight_sends += weight_copy(own_parts(hf), g, hf, lane, whom)
    for copy in weight_sends:
        copy.start()

    def slot_rows(h, q, ry, count=1):
        return xy.at[pl.ds(pl.multiple_of(((h * 4 + q) * ny + ry) * PAIR, PAIR), count * PAIR)]

    def near_copy(h, ry):
        sign = 1 - 2 * lax.rem(h + pz, 2)
        zt = lax.rem(z + sign * h + nz, nz)
        yt = lax.rem(y + ry, ny)
        to = yt * nh + lax.div(zt, 2)
        return pltpu.make_async_remote_copy(
            src_ref=pack.at[pl.ds(pl.multiple_of(to * PAIR, PAIR), PAIR)],
            dst_ref=slot_rows(h, 0, ry),
            send_sem=dsend,
            recv_sem=near_sem.at[h * ny + ry],
            device_id=device(yt, zt),
            device_id_type=MESH,
        )

    mine = pltpu.make_async_copy(
        pack.at[pl.ds(pl.multiple_of(lax.div(ei, 4) * PAIR, PAIR), PAIR)],
        slot_rows(0, 0, 0),
        near_sem.at[0],
    )
    mine.start()
    for h in range(min(nh, 3)):
        for ry in range(ny):
            if h or ry:
                near_copy(h, ry).start()

    def hand_on(h, q, ry, whom, to_q, send_sem, recv_sem):
        return pltpu.make_async_remote_copy(
            src_ref=slot_rows(h, q, ry),
            dst_ref=slot_rows(h, to_q, ry),
            send_sem=send_sem,
            recv_sem=recv_sem,
            device_id=whom,
            device_id_type=MESH,
        )

    def arrived(ref, sem):
        pltpu.make_async_copy(ref, ref, sem).wait()

    def pass_near(h, ry):
        arrived(slot_rows(h, 0, ry), near_sem.at[h * ny + ry])
        hand_on(h, 0, ry, mate, 1, psend, pair_sem.at[h * ny + ry]).start()
        hand_on(h, 0, ry, sib, 2, ssend, sib_sem.at[h, 0]).start()

    def pass_pair(h, ry):
        arrived(slot_rows(h, 1, ry), pair_sem.at[h * ny + ry])
        hand_on(h, 1, ry, sib, 3, ssend, sib_sem.at[h, 1]).start()

    def pass_weights(lane, hf, owner, whom):
        for i, ref in enumerate(weight_parts(owner, hf)):
            arrived(ref, wrecv.at[lane, hf, i])
        copies = weight_copy(weight_parts(owner, hf), owner, hf, 2, whom)
        for copy in copies:
            copy.start()
        return copies

    last = nh - 1
    for h in range(nh):
        for ry in range(ny):
            pass_near(h, ry)
        if 3 <= h + 2 < nh:
            for ry in range(ny):
                near_copy(h + 2, ry).start()
        if h:
            for ry in range(ny):
                pass_pair(h - 1, ry)
        if h == min(2, last):
            weight_sends += pass_weights(0, 0, g_left, right)
            weight_sends += pass_weights(1, 1, g_right, left)
    for h in range(last):
        for q in range(2):
            arrived(slot_rows(h, 2 + q, 0, ny), sib_sem.at[h, q])
    for copy in own_copies:
        copy.wait()
    for lane, hf, owner in (
        (0, 1, g_left),
        (1, 0, g_right),
        (2, 0, g_opp),
        (2, 1, g_opp),
    ):
        for i, ref in enumerate(weight_parts(owner, hf)):
            arrived(ref, wrecv.at[lane, hf, i])

    def z_copy(h):
        return pltpu.make_async_remote_copy(
            src_ref=zbuf.at[pl.ds(pl.multiple_of(h * batch + batch // 2, PAIR), batch // 2)],
            dst_ref=zrecv.at[pl.ds(pl.multiple_of(h * (batch // 2), PAIR), batch // 2)],
            send_sem=zsend.at[h],
            recv_sem=zwait.at[h],
            device_id=sib,
            device_id_type=MESH,
        )

    def rows_of(h):
        return pl.ds(pl.multiple_of(h * batch, batch), batch)

    def activations(h):
        rows = rows_of(h)
        pre = jnp.zeros((batch, hid), jnp.float32)
        up = jnp.zeros((batch, hid), jnp.float32)
        err = jnp.zeros((batch, hid), jnp.float32)
        for at in range(0, feat, kc):
            block = xy[rows, at : at + kc]
            pre += dot(block, wgu[0, at : at + kc])
            up += dot(block, wgu[1, at : at + kc])
            err += lax.dot_general(
                block,
                wd[:, at : at + kc],
                (((1,), (1,)), ((), ())),
                preferred_element_type=jnp.float32,
            )
        pre = pre.reshape(batch // PAIR, PAIR, hid)[:, :CAP]
        up = up.reshape(batch // PAIR, PAIR, hid)[:, :CAP]
        err = err.reshape(batch // PAIR, PAIR, hid)[:, CAP:]
        sig = jax.nn.sigmoid(pre)
        active = pre * sig * up
        d_gate = err * up * sig * (1.0 + pre * (1.0 - sig))
        d_up = err * pre * sig
        none = jnp.zeros_like(active)
        spread = jnp.concatenate(
            [
                jnp.concatenate([d_gate, d_up, none], axis=2),
                jnp.concatenate([none, none, active], axis=2),
            ],
            axis=1,
        )
        spread = spread.reshape(batch, 3 * hid).astype(jnp.bfloat16)
        return spread, active.reshape(batch // 2, hid).astype(jnp.bfloat16)

    def weight_grad(h, owner, spread):
        at = pl.ds(pl.multiple_of(owner * part, 128), part)
        return gacc[at] + lax.dot_general(
            xy[rows_of(h), at],
            spread,
            (((0,), (0,)), ((), ())),
            preferred_element_type=jnp.float32,
        )

    def project(h, act):
        kz = 256 if lanes % 256 == 0 else 128
        for at in range(0, lanes, kz):
            low = dot(act, wd[:, at : at + kz])
            top = dot(act, wd[:, lanes + at : lanes + at + kz])
            both = jnp.concatenate(
                [
                    low.reshape(batch // PAIR, CAP, kz),
                    top.reshape(batch // PAIR, CAP, kz),
                ],
                axis=1,
            )
            zbuf[rows_of(h), at : at + kz] = both.reshape(batch, kz).astype(jnp.bfloat16)
        z_copy(h).start()

    each = -(-ny // max(1, last - 1))

    def step(h, carry):
        spread, act = activations(h)
        for owner in range(4):
            gacc[owner * part : (owner + 1) * part] = weight_grad(h, owner, spread)
        project(h, act)
        for ry in range(ny):

            @pl.when(h == ry // each)
            def _(ry=ry):
                pass_pair(last, ry)

        return carry

    lax.fori_loop(0, last, step, 0)
    for q in range(2):
        arrived(slot_rows(last, 2 + q, 0, ny), sib_sem.at[last, q])

    def own_rows(owner):
        return pl.ds(pl.multiple_of(owner * part, 128), part)

    def grad_copy(k, src, dst, whom):
        return pltpu.make_async_remote_copy(
            src_ref=src,
            dst_ref=dst,
            send_sem=rsend.at[k],
            recv_sem=rwait.at[k],
            device_id=whom,
            device_id_type=MESH,
        )

    grad_sends = [
        grad_copy(0, gs.at[0, 0], part_l, right),
        grad_copy(1, gs.at[0, 1], part_r, left),
        grad_copy(2, gs.at[1, 1], from_l.at[1], right),
        grad_copy(3, gs.at[2, 0], from_r.at[0], left),
        grad_copy(4, gs.at[1, 0], from_l.at[0], right),
        grad_copy(5, gs.at[2, 1], from_r.at[1], left),
    ]
    spread, act = activations(last)
    wide = gacc.shape[1] // 2
    for slot, owner, sent in ((0, g_opp, ((0, 0), (1, 1))), (1, g_right, ((2, 1),)), (2, g_left, ((3, 0),))):
        full = weight_grad(last, owner, spread)
        for k, hf in sent:
            gs[slot, hf] = full[:, hf * wide : (hf + 1) * wide].astype(jnp.bfloat16)
            grad_sends[k].start()
        if slot:
            hf = 1 - sent[0][1]
            gacc[own_rows(owner), hf * wide : (hf + 1) * wide] = full[
                :, hf * wide : (hf + 1) * wide
            ]

    def o_copy(h, q, ry):
        ys = lax.rem(y - ry + ny, ny)
        if q == 0:
            zs = lax.rem(z + (2 * pz - 1) * h + nz, nz)
        else:
            zs = lax.rem(z + (1 - 2 * pz) * (1 + h) + nz, nz)
        return pltpu.make_async_remote_copy(
            src_ref=sbuf.at[pl.ds(pl.multiple_of(((h * 2 + q) * ny + ry) * PAIR, PAIR), PAIR)],
            dst_ref=orecv.at[pl.ds(pl.multiple_of((pz * experts + lax.div(ei, 4)) * PAIR, PAIR), PAIR)],
            send_sem=osend,
            recv_sem=owait,
            device_id=device(ys, zs),
            device_id_type=MESH,
        )

    here = pl.ds(
        pl.multiple_of((pz * experts + lax.div(ei, 4)) * PAIR, PAIR), PAIR
    )

    def send_back(h):
        z_copy(h).wait_recv()
        a, b = h * batch, h * (batch // 2)
        total = zbuf[a : a + batch // 2].astype(jnp.float32) + zrecv[
            b : b + batch // 2
        ].astype(jnp.float32)
        sbuf[b : b + batch // 2] = total.astype(jnp.bfloat16)
        for q in range(2):
            for ry in range(ny):
                if h or q or ry:
                    o_copy(h, q, ry).start()
                else:
                    pltpu.make_async_copy(
                        sbuf.at[pl.ds(0, PAIR)], orecv.at[here], owait
                    ).start()

    project(last, act)
    for h in range(last):
        send_back(h)
    gacc[own_rows(g)] = weight_grad(last, g, spread)
    send_back(last)

    for k, (came, slot, hf, owner) in enumerate(
        ((part_l, 1, 0, g_right), (part_r, 2, 1, g_left))
    ):
        arrived(came, rwait.at[k])
        gs[slot, hf] = (
            gacc[own_rows(owner), hf * wide : (hf + 1) * wide]
            + came[...].astype(jnp.float32)
        ).astype(jnp.bfloat16)
        grad_sends[4 + k].start()

    arrived(orecv, owait)
    for side in range(2):
        done = jnp.zeros((rows_t, lanes), jnp.float32)
        for which in range(2):
            part_o = orecv[which * experts * PAIR : (which + 1) * experts * PAIR]
            part_o = part_o.astype(jnp.float32).reshape(experts, PAIR, lanes)
            part_o = part_o[:, side * CAP : (side + 1) * CAP].reshape(slots, lanes)
            part_o = part_o.astype(jnp.bfloat16)
            done += dot(comb[0], part_o) + dot(comb[1], part_o)
        out[:, side * lanes : (side + 1) * lanes] = done.astype(jnp.bfloat16)

    totals = []
    for first, second, hf in ((4, 3, 0), (2, 5, 1)):
        arrived(from_l.at[hf], rwait.at[first])
        arrived(from_r.at[hf], rwait.at[second])
        totals.append(
            gacc[own_rows(g), hf * wide : (hf + 1) * wide]
            + from_l[hf].astype(jnp.float32)
            + from_r[hf].astype(jnp.float32)
        )
    gpair[0] = totals[0][:, :hid]
    gpair[1, :, : hid // 2] = totals[0][:, hid:]
    gpair[1, :, hid // 2 :] = totals[1][:, : hid // 2]
    gdown[...] = totals[1][:, hid // 2 :].T

    for copy in weight_sends + grad_sends:
        copy.wait_send()
    for h in range(nh):
        z_copy(h).wait_send()
    count = nh * ny
    arrived(xy.at[pl.ds(0, (count - 1) * PAIR)], dsend)
    arrived(xy.at[pl.ds(0, count * PAIR)], psend)
    arrived(xy.at[pl.ds(0, 2 * count * PAIR)], ssend)
    arrived(sbuf.at[pl.ds(0, (2 * count - 1) * PAIR)], osend)


def experts_step(tokens, cotangent, expert_ids, gate_weights, pair_own, down_own):
    shards = lax.axis_size("expert")
    ny, nz = NY, shards // (2 * NY)
    nh = nz // 2
    experts = shards // SPLIT
    rows, feat = tokens.shape
    hid = down_own.shape[0]
    part, lanes, wide = feat // 4, feat // 2, 3 * hid // 2
    slots = experts * CAP
    batch = 4 * ny * PAIR
    vmem = pl.BlockSpec(memory_space=pltpu.VMEM)
    hbm = pl.BlockSpec(memory_space=pltpu.HBM)
    bf, f32 = jnp.bfloat16, jnp.float32
    dma = pltpu.SemaphoreType.DMA
    return pl.pallas_call(
        functools.partial(moe_kernel, ny, nz),
        out_shape=(
            jax.ShapeDtypeStruct((rows, feat), bf),
            jax.ShapeDtypeStruct((2, part, hid), f32),
            jax.ShapeDtypeStruct((hid, part), f32),
        ),
        in_specs=[hbm] * 6,
        out_specs=(vmem, vmem, vmem),
        scratch_shapes=[
            pltpu.VMEM((rows, feat), bf),
            pltpu.VMEM((rows, feat), bf),
            pltpu.VMEM((TOP, rows), jnp.int32),
            pltpu.VMEM((TOP, rows), f32),
            pltpu.VMEM((experts * PAIR, feat), bf),
            pltpu.VMEM((2, rows, slots), bf),
            pltpu.VMEM((nh * batch, feat), bf),
            pltpu.VMEM((2, feat, hid), bf),
            pltpu.VMEM((hid, feat), bf),
            pltpu.VMEM((feat, 3 * hid), f32),
            pltpu.VMEM((3, 2, part, wide), bf),
            pltpu.VMEM((part, wide), bf),
            pltpu.VMEM((part, wide), bf),
            pltpu.VMEM((2, part, wide), bf),
            pltpu.VMEM((2, part, wide), bf),
            pltpu.VMEM((nh * batch, lanes), bf),
            pltpu.VMEM((nh * batch // 2, lanes), bf),
            pltpu.VMEM((nh * batch // 2, lanes), bf),
            pltpu.VMEM((2 * experts * PAIR, lanes), bf),
            dma((2,)),
            dma((3, 2, 2)),
            dma((3, 2, 2)),
            dma,
            dma,
            dma,
            dma((nh * ny,)),
            dma((nh * ny,)),
            dma((nh, 2)),
            dma((nh,)),
            dma((nh,)),
            dma,
            dma,
            dma((6,)),
            dma((6,)),
            dma((4,)),
        ],
        compiler_params=pltpu.CompilerParams(
            collective_id=0,
            has_side_effects=True,
            vmem_limit_bytes=46 * 1024 * 1024,
        ),
        cost_estimate=pl.CostEstimate(
            flops=8_000_000_000, bytes_accessed=10_000_000, transcendentals=200_000
        ),
    )(
        *(
            pltpu.with_memory_space_constraint(a, pltpu.HBM)
            for a in (
                tokens,
                cotangent,
                expert_ids.T,
                gate_weights.T,
                pair_own,
                down_own,
            )
        )
    )


def body(
    tokens,
    cotangent,
    expert_ids,
    gate_weights,
    gate_up,
    down_proj,
    gate_up_first,
    gate_up_second,
    down_first,
    down_second,
):
    layer_out, own_pair, own_down = experts_step(
        tokens, cotangent, expert_ids, gate_weights, gate_up[0], down_proj[0]
    )
    gate_up_new, gate_up_first_new, gate_up_second_new = adamw_update(
        gate_up, own_pair[None], gate_up_first, gate_up_second
    )
    down_new, down_first_new, down_second_new = adamw_update(
        down_proj, own_down[None], down_first, down_second
    )
    return (
        layer_out,
        gate_up_new,
        down_new,
        gate_up_first_new,
        gate_up_second_new,
        down_first_new,
        down_second_new,
    )


def solution(mesh):
    return jax.shard_map(
        body,
        mesh=mesh,
        in_specs=(
            P(("dp", "expert"), None),
            P(("dp", "expert"), None),
            P(("dp", "expert"), None),
            P(("dp", "expert"), None),
            P("expert", None, "dp", None),
            P("expert", None, "dp"),
            P("expert", None, "dp", None),
            P("expert", None, "dp", None),
            P("expert", None, "dp"),
            P("expert", None, "dp"),
        ),
        out_specs=(
            P(("dp", "expert"), None),
            P("expert", None, "dp", None),
            P("expert", None, "dp"),
            P("expert", None, "dp", None),
            P("expert", None, "dp", None),
            P("expert", None, "dp"),
            P("expert", None, "dp"),
        ),
        check_vma=False,
    )
```

```python
import functools

import jax
import jax.numpy as jnp
from jax import lax
from jax.experimental import pallas as pl
from jax.experimental.pallas import tpu as pltpu
from jax.sharding import PartitionSpec as P

TOP = 6
SPLIT = 4
CAP = 8
PAIR = 2 * CAP
NY = 4
MESH = pl.DeviceIdType.MESH

beta_one = 0.9
beta_two = 0.95
learn_rate = 0.001
decay_rate = 0.1
step_count = 10.0
epsilon = 1e-08


def adamw_update(weight, gradient, first, second):
    first_new = beta_one * first + (1.0 - beta_one) * gradient
    second_new = beta_two * second + (1.0 - beta_two) * gradient * gradient
    first_hat = first_new / (1.0 - beta_one**step_count)
    second_hat = second_new / (1.0 - beta_two**step_count)
    weight_float = weight.astype(jnp.float32)
    updated = weight_float - learn_rate * (
        first_hat / (jnp.sqrt(second_hat) + epsilon) + decay_rate * weight_float
    )
    return (updated.astype(jnp.bfloat16), first_new, second_new)


def dot(left, right):
    return jnp.dot(left, right, preferred_element_type=jnp.float32)


def chunk_of(size):
    return 512 if size % 512 == 0 else 128


def moe_kernel(
    ny,
    nz,
    tokens_in,
    cot_in,
    ids_in,
    gates_in,
    gu_own,
    dn_own,
    out,
    gpair,
    gdown,
    tokens,
    cot,
    ids,
    gates,
    pack,
    comb,
    xy,
    wgu,
    wd,
    gacc,
    gs,
    part_l,
    part_r,
    from_l,
    from_r,
    zbuf,
    zrecv,
    sbuf,
    orecv,
    own_sem,
    wsend,
    wrecv,
    dsend,
    psend,
    ssend,
    near_sem,
    pair_sem,
    sib_sem,
    zsend,
    zwait,
    osend,
    owait,
    rsend,
    rwait,
    in_sem,
):
    nh = nz // 2
    experts = ny * nh
    slots = experts * CAP
    rows_t, feat = tokens.shape
    part = feat // 4
    hid = wd.shape[0]
    half, hhid = part // 2, hid // 2
    lanes = feat // 2
    batch = 4 * ny * PAIR

    g = lax.axis_index("dp")
    ei = lax.axis_index("expert")
    core = lax.rem(ei, 2)
    chip = lax.div(ei, 2)
    z = lax.rem(chip, nz)
    y = lax.div(chip, nz)
    pz = lax.rem(z, 2)
    right, left = (lax.rem(g + 1, 4), ei), (lax.rem(g + 3, 4), ei)
    sib = (g, ei + 1 - 2 * core)
    mate = (g, ei + 2 - 4 * pz)

    def device(yy, zz):
        return (g, (yy * nz + zz) * 2 + core)

    loads = [
        pltpu.make_async_copy(src, dst, in_sem.at[i])
        for i, (src, dst) in enumerate(
            ((ids_in, ids), (gates_in, gates), (tokens_in, tokens), (cot_in, cot))
        )
    ]
    for copy in loads:
        copy.start()

    barrier = pltpu.get_barrier_semaphore()

    def greet(step, carry):
        other = lax.rem(chip + step, ny * nz)
        pl.semaphore_signal(
            barrier, inc=1, device_id=(g, other * 2 + core), device_id_type=MESH
        )
        return carry

    for who in (left, right, sib):
        pl.semaphore_signal(barrier, inc=1, device_id=who, device_id_type=MESH)
    lax.fori_loop(1, ny * nz, greet, 0)

    own_copies = [
        pltpu.make_async_copy(
            gu_own, wgu.at[:, pl.ds(pl.multiple_of(g * part, 128), part)], own_sem.at[0]
        ),
        pltpu.make_async_copy(
            dn_own, wd.at[:, pl.ds(pl.multiple_of(g * part, 128), part)], own_sem.at[1]
        ),
    ]
    for copy in own_copies:
        copy.start()
    for copy in loads:
        copy.wait()

    row = lax.broadcasted_iota(jnp.int32, (slots, rows_t), 0)
    named = jnp.zeros((slots, rows_t), jnp.float32)
    weight = jnp.zeros((slots, rows_t), jnp.float32)
    for k in range(TOP):
        hit = ids[k : k + 1] == row // CAP
        named = jnp.where(hit, 1.0, named)
        weight = jnp.where(hit, gates[k : k + 1], weight)
    earlier = lax.broadcasted_iota(jnp.int32, (rows_t, rows_t), 0) < lax.broadcasted_iota(
        jnp.int32, (rows_t, rows_t), 1
    )
    before = dot(
        named.astype(jnp.bfloat16), jnp.where(earlier, 1.0, 0.0).astype(jnp.bfloat16)
    )
    chosen = jnp.where(before == (row % CAP).astype(jnp.float32), named, 0.0)
    scale = chosen * weight
    pick = chosen.astype(jnp.bfloat16)
    slot_weight = jnp.sum(scale, axis=1, keepdims=True)
    back = scale.T
    high = back.astype(jnp.bfloat16)
    comb[0] = high
    comb[1] = (back - high.astype(jnp.float32)).astype(jnp.bfloat16)
    kc = chunk_of(feat)
    for at in range(0, feat, kc):
        xs = dot(pick, tokens[:, at : at + kc]).reshape(experts, CAP, kc)
        ys = (dot(pick, cot[:, at : at + kc]) * slot_weight).reshape(experts, CAP, kc)
        both = jnp.concatenate([xs, ys], axis=1).reshape(experts * PAIR, kc)
        pack[:, at : at + kc] = both.astype(jnp.bfloat16)

    gacc[...] = jnp.zeros_like(gacc)

    pl.semaphore_wait(barrier, ny * nz + 2)

    def weight_parts(owner, hf):
        return (
            wgu.at[:, pl.ds(pl.multiple_of(owner * part + hf * half, 64), half)],
            wd.at[pl.ds(hf * hhid, hhid), pl.ds(pl.multiple_of(owner * part, 128), part)],
        )

    def weight_copy(src_refs, owner, hf, lane, whom):
        return [
            pltpu.make_async_remote_copy(
                src_ref=s,
                dst_ref=d,
                send_sem=wsend.at[lane, hf, i],
                recv_sem=wrecv.at[lane, hf, i],
                device_id=whom,
                device_id_type=MESH,
            )
            for i, (s, d) in enumerate(
                zip(src_refs, weight_parts(owner, hf), strict=True)
            )
        ]

    def own_parts(hf):
        return (
            gu_own.at[:, pl.ds(hf * half, half)],
            dn_own.at[pl.ds(hf * hhid, hhid)],
        )

    g_left, g_right, g_opp = lax.rem(g + 3, 4), lax.rem(g + 1, 4), lax.rem(g + 2, 4)
    weight_sends = []
    for turn in range(2):
        for lane, whom in ((0, right), (1, left)):
            hf = turn if lane == 0 else 1 - turn
            weight_sends += weight_copy(own_parts(hf), g, hf, lane, whom)
    for copy in weight_sends:
        copy.start()

    def slot_rows(h, q, ry, count=1):
        return xy.at[pl.ds(pl.multiple_of(((h * 4 + q) * ny + ry) * PAIR, PAIR), count * PAIR)]

    def near_copy(h, ry):
        sign = 1 - 2 * lax.rem(h + pz, 2)
        zt = lax.rem(z + sign * h + nz, nz)
        yt = lax.rem(y + ry, ny)
        to = yt * nh + lax.div(zt, 2)
        return pltpu.make_async_remote_copy(
            src_ref=pack.at[pl.ds(pl.multiple_of(to * PAIR, PAIR), PAIR)],
            dst_ref=slot_rows(h, 0, ry),
            send_sem=dsend,
            recv_sem=near_sem.at[h * ny + ry],
            device_id=device(yt, zt),
            device_id_type=MESH,
        )

    mine = pltpu.make_async_copy(
        pack.at[pl.ds(pl.multiple_of(lax.div(ei, 4) * PAIR, PAIR), PAIR)],
        slot_rows(0, 0, 0),
        near_sem.at[0],
    )
    mine.start()
    for h in range(min(nh, 3)):
        for ry in range(ny):
            if h or ry:
                near_copy(h, ry).start()

    def hand_on(h, q, ry, whom, to_q, send_sem, recv_sem):
        return pltpu.make_async_remote_copy(
            src_ref=slot_rows(h, q, ry),
            dst_ref=slot_rows(h, to_q, ry),
            send_sem=send_sem,
            recv_sem=recv_sem,
            device_id=whom,
            device_id_type=MESH,
        )

    def arrived(ref, sem):
        pltpu.make_async_copy(ref, ref, sem).wait()

    def pass_near(h, ry):
        arrived(slot_rows(h, 0, ry), near_sem.at[h * ny + ry])
        hand_on(h, 0, ry, mate, 1, psend, pair_sem.at[h * ny + ry]).start()
        hand_on(h, 0, ry, sib, 2, ssend, sib_sem.at[h, 0]).start()

    def pass_pair(h, ry):
        arrived(slot_rows(h, 1, ry), pair_sem.at[h * ny + ry])
        hand_on(h, 1, ry, sib, 3, ssend, sib_sem.at[h, 1]).start()

    def pass_weights(lane, hf, owner, whom):
        for i, ref in enumerate(weight_parts(owner, hf)):
            arrived(ref, wrecv.at[lane, hf, i])
        copies = weight_copy(weight_parts(owner, hf), owner, hf, 2, whom)
        for copy in copies:
            copy.start()
        return copies

    last = nh - 1
    for h in range(nh):
        for ry in range(ny):
            pass_near(h, ry)
        if 3 <= h + 2 < nh:
            for ry in range(ny):
                near_copy(h + 2, ry).start()
        if h:
            for ry in range(ny):
                pass_pair(h - 1, ry)
        if h == min(2, last):
            weight_sends += pass_weights(0, 0, g_left, right)
            weight_sends += pass_weights(1, 1, g_right, left)
    for h in range(last):
        for q in range(2):
            arrived(slot_rows(h, 2 + q, 0, ny), sib_sem.at[h, q])
    for copy in own_copies:
        copy.wait()
    for lane, hf, owner in (
        (0, 1, g_left),
        (1, 0, g_right),
        (2, 0, g_opp),
        (2, 1, g_opp),
    ):
        for i, ref in enumerate(weight_parts(owner, hf)):
            arrived(ref, wrecv.at[lane, hf, i])

    def z_copy(h):
        return pltpu.make_async_remote_copy(
            src_ref=zbuf.at[pl.ds(pl.multiple_of(h * batch + batch // 2, PAIR), batch // 2)],
            dst_ref=zrecv.at[pl.ds(pl.multiple_of(h * (batch // 2), PAIR), batch // 2)],
            send_sem=zsend.at[h],
            recv_sem=zwait.at[h],
            device_id=sib,
            device_id_type=MESH,
        )

    def rows_of(h):
        return pl.ds(pl.multiple_of(h * batch, batch), batch)

    def activations(h):
        rows = rows_of(h)
        pre = jnp.zeros((batch, hid), jnp.float32)
        up = jnp.zeros((batch, hid), jnp.float32)
        err = jnp.zeros((batch, hid), jnp.float32)
        for at in range(0, feat, kc):
            block = xy[rows, at : at + kc]
            pre += dot(block, wgu[0, at : at + kc])
            up += dot(block, wgu[1, at : at + kc])
            err += lax.dot_general(
                block,
                wd[:, at : at + kc],
                (((1,), (1,)), ((), ())),
                preferred_element_type=jnp.float32,
            )
        pre = pre.reshape(batch // PAIR, PAIR, hid)[:, :CAP]
        up = up.reshape(batch // PAIR, PAIR, hid)[:, :CAP]
        err = err.reshape(batch // PAIR, PAIR, hid)[:, CAP:]
        sig = jax.nn.sigmoid(pre)
        active = pre * sig * up
        d_gate = err * up * sig * (1.0 + pre * (1.0 - sig))
        d_up = err * pre * sig
        none = jnp.zeros_like(active)
        spread = jnp.concatenate(
            [
                jnp.concatenate([d_gate, d_up, none], axis=2),
                jnp.concatenate([none, none, active], axis=2),
            ],
            axis=1,
        )
        spread = spread.reshape(batch, 3 * hid).astype(jnp.bfloat16)
        return spread, active.reshape(batch // 2, hid).astype(jnp.bfloat16)

    def weight_grad(h, owner, spread):
        at = pl.ds(pl.multiple_of(owner * part, 128), part)
        return gacc[at] + lax.dot_general(
            xy[rows_of(h), at],
            spread,
            (((0,), (0,)), ((), ())),
            preferred_element_type=jnp.float32,
        )

    def project(h, act):
        kz = 256 if lanes % 256 == 0 else 128
        for at in range(0, lanes, kz):
            low = dot(act, wd[:, at : at + kz])
            top = dot(act, wd[:, lanes + at : lanes + at + kz])
            both = jnp.concatenate(
                [
                    low.reshape(batch // PAIR, CAP, kz),
                    top.reshape(batch // PAIR, CAP, kz),
                ],
                axis=1,
            )
            zbuf[rows_of(h), at : at + kz] = both.reshape(batch, kz).astype(jnp.bfloat16)
        z_copy(h).start()

    def pass_some(h, piece):
        for ry in range(ny):
            at = min(ry, 2 * last - 1)

            @pl.when(h * 2 + piece == at)
            def _(ry=ry):
                pass_pair(last, ry)

    def step(h, carry):
        spread, act = activations(h)
        pass_some(h, 0)
        for owner in range(4):
            gacc[owner * part : (owner + 1) * part] = weight_grad(h, owner, spread)
        project(h, act)
        pass_some(h, 1)
        return carry

    lax.fori_loop(0, last, step, 0)
    for q in range(2):
        arrived(slot_rows(last, 2 + q, 0, ny), sib_sem.at[last, q])

    def own_rows(owner):
        return pl.ds(pl.multiple_of(owner * part, 128), part)

    def grad_copy(k, src, dst, whom):
        return pltpu.make_async_remote_copy(
            src_ref=src,
            dst_ref=dst,
            send_sem=rsend.at[k],
            recv_sem=rwait.at[k],
            device_id=whom,
            device_id_type=MESH,
        )

    grad_sends = [
        grad_copy(0, gs.at[0, 0], part_l, right),
        grad_copy(1, gs.at[0, 1], part_r, left),
        grad_copy(2, gs.at[1, 1], from_l.at[1], right),
        grad_copy(3, gs.at[2, 0], from_r.at[0], left),
        grad_copy(4, gs.at[1, 0], from_l.at[0], right),
        grad_copy(5, gs.at[2, 1], from_r.at[1], left),
    ]
    spread, act = activations(last)
    wide = gacc.shape[1] // 2
    for slot, owner, sent in ((0, g_opp, ((0, 0), (1, 1))), (1, g_right, ((2, 1),)), (2, g_left, ((3, 0),))):
        full = weight_grad(last, owner, spread)
        for k, hf in sent:
            gs[slot, hf] = full[:, hf * wide : (hf + 1) * wide].astype(jnp.bfloat16)
            grad_sends[k].start()
        if slot:
            hf = 1 - sent[0][1]
            gacc[own_rows(owner), hf * wide : (hf + 1) * wide] = full[
                :, hf * wide : (hf + 1) * wide
            ]

    def o_copy(h, q, ry):
        ys = lax.rem(y - ry + ny, ny)
        if q == 0:
            zs = lax.rem(z + (2 * pz - 1) * h + nz, nz)
        else:
            zs = lax.rem(z + (1 - 2 * pz) * (1 + h) + nz, nz)
        return pltpu.make_async_remote_copy(
            src_ref=sbuf.at[pl.ds(pl.multiple_of(((h * 2 + q) * ny + ry) * PAIR, PAIR), PAIR)],
            dst_ref=orecv.at[pl.ds(pl.multiple_of((pz * experts + lax.div(ei, 4)) * PAIR, PAIR), PAIR)],
            send_sem=osend,
            recv_sem=owait,
            device_id=device(ys, zs),
            device_id_type=MESH,
        )

    here = pl.ds(
        pl.multiple_of((pz * experts + lax.div(ei, 4)) * PAIR, PAIR), PAIR
    )

    def send_back(h):
        z_copy(h).wait_recv()
        a, b = h * batch, h * (batch // 2)
        total = zbuf[a : a + batch // 2].astype(jnp.float32) + zrecv[
            b : b + batch // 2
        ].astype(jnp.float32)
        sbuf[b : b + batch // 2] = total.astype(jnp.bfloat16)
        for q in range(2):
            for ry in range(ny):
                if h or q or ry:
                    o_copy(h, q, ry).start()
                else:
                    pltpu.make_async_copy(
                        sbuf.at[pl.ds(0, PAIR)], orecv.at[here], owait
                    ).start()

    project(last, act)
    for h in range(last):
        send_back(h)
    gacc[own_rows(g)] = weight_grad(last, g, spread)
    send_back(last)

    for k, (came, slot, hf, owner) in enumerate(
        ((part_l, 1, 0, g_right), (part_r, 2, 1, g_left))
    ):
        arrived(came, rwait.at[k])
        gs[slot, hf] = (
            gacc[own_rows(owner), hf * wide : (hf + 1) * wide]
            + came[...].astype(jnp.float32)
        ).astype(jnp.bfloat16)
        grad_sends[4 + k].start()

    for k, came, hf in ((3, from_r, 0), (2, from_l, 1)):
        arrived(came.at[hf], rwait.at[k])
        cols = slice(hf * wide, (hf + 1) * wide)
        gacc[own_rows(g), cols] = gacc[own_rows(g), cols] + came[hf].astype(jnp.float32)

    arrived(orecv, owait)
    for side in range(2):
        done = jnp.zeros((rows_t, lanes), jnp.float32)
        for which in range(2):
            part_o = orecv[which * experts * PAIR : (which + 1) * experts * PAIR]
            part_o = part_o.astype(jnp.float32).reshape(experts, PAIR, lanes)
            part_o = part_o[:, side * CAP : (side + 1) * CAP].reshape(slots, lanes)
            part_o = part_o.astype(jnp.bfloat16)
            done += dot(comb[0], part_o) + dot(comb[1], part_o)
        out[:, side * lanes : (side + 1) * lanes] = done.astype(jnp.bfloat16)

    totals = []
    for k, came, hf in ((4, from_l, 0), (5, from_r, 1)):
        arrived(came.at[hf], rwait.at[k])
        cols = slice(hf * wide, (hf + 1) * wide)
        totals.append(gacc[own_rows(g), cols] + came[hf].astype(jnp.float32))
    gpair[0] = totals[0][:, :hid]
    gpair[1, :, : hid // 2] = totals[0][:, hid:]
    gpair[1, :, hid // 2 :] = totals[1][:, : hid // 2]
    gdown[...] = totals[1][:, hid // 2 :].T

    for copy in weight_sends + grad_sends:
        copy.wait_send()
    for h in range(nh):
        z_copy(h).wait_send()
    count = nh * ny
    arrived(xy.at[pl.ds(0, (count - 1) * PAIR)], dsend)
    arrived(xy.at[pl.ds(0, count * PAIR)], psend)
    arrived(xy.at[pl.ds(0, 2 * count * PAIR)], ssend)
    arrived(sbuf.at[pl.ds(0, (2 * count - 1) * PAIR)], osend)


def experts_step(tokens, cotangent, expert_ids, gate_weights, pair_own, down_own):
    shards = lax.axis_size("expert")
    ny, nz = NY, shards // (2 * NY)
    nh = nz // 2
    experts = shards // SPLIT
    rows, feat = tokens.shape
    hid = down_own.shape[0]
    part, lanes, wide = feat // 4, feat // 2, 3 * hid // 2
    slots = experts * CAP
    batch = 4 * ny * PAIR
    vmem = pl.BlockSpec(memory_space=pltpu.VMEM)
    hbm = pl.BlockSpec(memory_space=pltpu.HBM)
    bf, f32 = jnp.bfloat16, jnp.float32
    dma = pltpu.SemaphoreType.DMA
    return pl.pallas_call(
        functools.partial(moe_kernel, ny, nz),
        out_shape=(
            jax.ShapeDtypeStruct((rows, feat), bf),
            jax.ShapeDtypeStruct((2, part, hid), f32),
            jax.ShapeDtypeStruct((hid, part), f32),
        ),
        in_specs=[hbm] * 6,
        out_specs=(vmem, vmem, vmem),
        scratch_shapes=[
            pltpu.VMEM((rows, feat), bf),
            pltpu.VMEM((rows, feat), bf),
            pltpu.VMEM((TOP, rows), jnp.int32),
            pltpu.VMEM((TOP, rows), f32),
            pltpu.VMEM((experts * PAIR, feat), bf),
            pltpu.VMEM((2, rows, slots), bf),
            pltpu.VMEM((nh * batch, feat), bf),
            pltpu.VMEM((2, feat, hid), bf),
            pltpu.VMEM((hid, feat), bf),
            pltpu.VMEM((feat, 3 * hid), f32),
            pltpu.VMEM((3, 2, part, wide), bf),
            pltpu.VMEM((part, wide), bf),
            pltpu.VMEM((part, wide), bf),
            pltpu.VMEM((2, part, wide), bf),
            pltpu.VMEM((2, part, wide), bf),
            pltpu.VMEM((nh * batch, lanes), bf),
            pltpu.VMEM((nh * batch // 2, lanes), bf),
            pltpu.VMEM((nh * batch // 2, lanes), bf),
            pltpu.VMEM((2 * experts * PAIR, lanes), bf),
            dma((2,)),
            dma((3, 2, 2)),
            dma((3, 2, 2)),
            dma,
            dma,
            dma,
            dma((nh * ny,)),
            dma((nh * ny,)),
            dma((nh, 2)),
            dma((nh,)),
            dma((nh,)),
            dma,
            dma,
            dma((6,)),
            dma((6,)),
            dma((4,)),
        ],
        compiler_params=pltpu.CompilerParams(
            collective_id=0,
            has_side_effects=True,
            vmem_limit_bytes=46 * 1024 * 1024,
        ),
        cost_estimate=pl.CostEstimate(
            flops=8_000_000_000, bytes_accessed=10_000_000, transcendentals=200_000
        ),
    )(
        *(
            pltpu.with_memory_space_constraint(a, pltpu.HBM)
            for a in (
                tokens,
                cotangent,
                expert_ids.T,
                gate_weights.T,
                pair_own,
                down_own,
            )
        )
    )


def update_kernel(*refs):
    ins, outs, scratch, sem = refs[:9], refs[9:16], refs[16:22], refs[22]
    copies = [pltpu.make_async_copy(ins[8], outs[6], sem.at[0])]
    copies[0].start()
    for which in range(2):
        weight, gradient, first, second = ins[which * 4 : which * 4 + 4]
        kept, to = scratch[which * 3 : which * 3 + 3], outs[which * 3 : which * 3 + 3]
        rows = weight.shape[0]
        count = 8 if which == 0 else 4
        size = rows // count
        for at in range(0, rows, size):
            piece = slice(at, at + size)
            made = adamw_update(
                weight[piece], gradient[piece], first[piece], second[piece]
            )
            for value, keep, end in zip(made, kept, to, strict=True):
                keep[piece] = value
                copies.append(
                    pltpu.make_async_copy(
                        keep.at[pl.ds(at, size)],
                        end.at[pl.ds(at, size)],
                        sem.at[len(copies)],
                    )
                )
                copies[-1].start()
    for copy in copies:
        copy.wait()


def update(pair, down, layer_out):
    vmem = pl.BlockSpec(memory_space=pltpu.VMEM)
    hbm = pl.BlockSpec(memory_space=pltpu.HBM)
    kinds = []
    for group in (pair, down):
        for dtype in (jnp.bfloat16, jnp.float32, jnp.float32):
            kinds.append((group[0].shape, dtype))
    return pl.pallas_call(
        update_kernel,
        out_shape=tuple(
            jax.ShapeDtypeStruct(*kind)
            for kind in (*kinds, (layer_out.shape, layer_out.dtype))
        ),
        in_specs=[vmem] * 9,
        out_specs=(hbm,) * 7,
        scratch_shapes=[pltpu.VMEM(*kind) for kind in kinds]
        + [pltpu.SemaphoreType.DMA((37,))],
        compiler_params=pltpu.CompilerParams(vmem_limit_bytes=32 * 1024 * 1024),
        cost_estimate=pl.CostEstimate(
            flops=15_000_000, bytes_accessed=12_000_000, transcendentals=1_000_000
        ),
    )(*pair, *down, layer_out)


def body(
    tokens,
    cotangent,
    expert_ids,
    gate_weights,
    gate_up,
    down_proj,
    gate_up_first,
    gate_up_second,
    down_first,
    down_second,
):
    layer_out, own_pair, own_down = experts_step(
        tokens, cotangent, expert_ids, gate_weights, gate_up[0], down_proj[0]
    )

    def flat(a):
        return a.reshape(-1, a.shape[-1])

    pair = [flat(a) for a in (gate_up, own_pair, gate_up_first, gate_up_second)]
    down = [flat(a) for a in (down_proj, own_down, down_first, down_second)]
    made = update(pair, down, layer_out)
    pair_new = [a.reshape(gate_up.shape) for a in made[:3]]
    down_new = [a.reshape(down_proj.shape) for a in made[3:6]]
    return (
        made[6],
        pair_new[0],
        down_new[0],
        pair_new[1],
        pair_new[2],
        down_new[1],
        down_new[2],
    )


def solution(mesh):
    return jax.shard_map(
        body,
        mesh=mesh,
        in_specs=(
            P(("dp", "expert"), None),
            P(("dp", "expert"), None),
            P(("dp", "expert"), None),
            P(("dp", "expert"), None),
            P("expert", None, "dp", None),
            P("expert", None, "dp"),
            P("expert", None, "dp", None),
            P("expert", None, "dp", None),
            P("expert", None, "dp"),
            P("expert", None, "dp"),
        ),
        out_specs=(
            P(("dp", "expert"), None),
            P("expert", None, "dp", None),
            P("expert", None, "dp"),
            P("expert", None, "dp", None),
            P("expert", None, "dp", None),
            P("expert", None, "dp"),
            P("expert", None, "dp"),
        ),
        check_vma=False,
    )
```

```python
import functools

import jax
import jax.numpy as jnp
from jax import lax
from jax.experimental import pallas as pl
from jax.experimental.pallas import tpu as pltpu
from jax.sharding import PartitionSpec as P

TOP = 6
SPLIT = 4
CAP = 8
PAIR = 2 * CAP
NY = 4
MESH = pl.DeviceIdType.MESH

beta_one = 0.9
beta_two = 0.95
learn_rate = 0.001
decay_rate = 0.1
step_count = 10.0
epsilon = 1e-08


def adamw_update(weight, gradient, first, second):
    first_new = beta_one * first + (1.0 - beta_one) * gradient
    second_new = beta_two * second + (1.0 - beta_two) * gradient * gradient
    first_hat = first_new / (1.0 - beta_one**step_count)
    second_hat = second_new / (1.0 - beta_two**step_count)
    weight_float = weight.astype(jnp.float32)
    updated = weight_float - learn_rate * (
        first_hat / (jnp.sqrt(second_hat) + epsilon) + decay_rate * weight_float
    )
    return (updated.astype(jnp.bfloat16), first_new, second_new)


def dot(left, right):
    return jnp.dot(left, right, preferred_element_type=jnp.float32)


def chunk_of(size):
    return 512 if size % 512 == 0 else 128


def moe_kernel(
    ny,
    nz,
    tokens_in,
    cot_in,
    ids_in,
    gates_in,
    gu_own,
    dn_own,
    out,
    gpair,
    gdown,
    tokens,
    cot,
    ids,
    gates,
    pack,
    comb,
    xy,
    wgu,
    wd,
    gacc,
    gs,
    part_l,
    part_r,
    from_l,
    from_r,
    zbuf,
    zrecv,
    sbuf,
    orecv,
    own_sem,
    wsend,
    wrecv,
    dsend,
    psend,
    ssend,
    near_sem,
    pair_sem,
    sib_sem,
    zsend,
    zwait,
    osend,
    owait,
    rsend,
    rwait,
    in_sem,
):
    nh = nz // 2
    experts = ny * nh
    slots = experts * CAP
    rows_t, feat = tokens.shape
    part = feat // 4
    hid = wd.shape[0]
    half, hhid = part // 2, hid // 2
    lanes = feat // 2
    batch = 4 * ny * PAIR

    g = lax.axis_index("dp")
    ei = lax.axis_index("expert")
    core = lax.rem(ei, 2)
    chip = lax.div(ei, 2)
    z = lax.rem(chip, nz)
    y = lax.div(chip, nz)
    pz = lax.rem(z, 2)
    right, left = (lax.rem(g + 1, 4), ei), (lax.rem(g + 3, 4), ei)
    sib = (g, ei + 1 - 2 * core)
    mate = (g, ei + 2 - 4 * pz)

    def device(yy, zz):
        return (g, (yy * nz + zz) * 2 + core)

    loads = [
        pltpu.make_async_copy(src, dst, in_sem.at[i])
        for i, (src, dst) in enumerate(
            ((ids_in, ids), (gates_in, gates), (tokens_in, tokens), (cot_in, cot))
        )
    ]
    for copy in loads:
        copy.start()

    barrier = pltpu.get_barrier_semaphore()

    def greet(step, carry):
        other = lax.rem(chip + step, ny * nz)
        pl.semaphore_signal(
            barrier, inc=1, device_id=(g, other * 2 + core), device_id_type=MESH
        )
        return carry

    for who in (left, right, sib):
        pl.semaphore_signal(barrier, inc=1, device_id=who, device_id_type=MESH)
    lax.fori_loop(1, ny * nz, greet, 0)

    own_copies = [
        pltpu.make_async_copy(
            gu_own, wgu.at[:, pl.ds(pl.multiple_of(g * part, 128), part)], own_sem.at[0]
        ),
        pltpu.make_async_copy(
            dn_own, wd.at[:, pl.ds(pl.multiple_of(g * part, 128), part)], own_sem.at[1]
        ),
    ]
    for copy in own_copies:
        copy.start()
    for copy in loads:
        copy.wait()

    row = lax.broadcasted_iota(jnp.int32, (slots, rows_t), 0)
    named = jnp.zeros((slots, rows_t), jnp.float32)
    weight = jnp.zeros((slots, rows_t), jnp.float32)
    for k in range(TOP):
        hit = ids[k : k + 1] == row // CAP
        named = jnp.where(hit, 1.0, named)
        weight = jnp.where(hit, gates[k : k + 1], weight)
    earlier = lax.broadcasted_iota(jnp.int32, (rows_t, rows_t), 0) < lax.broadcasted_iota(
        jnp.int32, (rows_t, rows_t), 1
    )
    before = dot(
        named.astype(jnp.bfloat16), jnp.where(earlier, 1.0, 0.0).astype(jnp.bfloat16)
    )
    chosen = jnp.where(before == (row % CAP).astype(jnp.float32), named, 0.0)
    scale = chosen * weight
    pick = chosen.astype(jnp.bfloat16)
    slot_weight = jnp.sum(scale, axis=1, keepdims=True)
    back = scale.T
    high = back.astype(jnp.bfloat16)
    comb[0] = high
    comb[1] = (back - high.astype(jnp.float32)).astype(jnp.bfloat16)
    kc = chunk_of(feat)
    for at in range(0, feat, kc):
        xs = dot(pick, tokens[:, at : at + kc]).reshape(experts, CAP, kc)
        ys = (dot(pick, cot[:, at : at + kc]) * slot_weight).reshape(experts, CAP, kc)
        both = jnp.concatenate([xs, ys], axis=1).reshape(experts * PAIR, kc)
        pack[:, at : at + kc] = both.astype(jnp.bfloat16)

    gacc[...] = jnp.zeros_like(gacc)

    pl.semaphore_wait(barrier, ny * nz + 2)

    def weight_parts(owner, hf):
        return (
            wgu.at[:, pl.ds(pl.multiple_of(owner * part + hf * half, 64), half)],
            wd.at[pl.ds(hf * hhid, hhid), pl.ds(pl.multiple_of(owner * part, 128), part)],
        )

    def weight_copy(src_refs, owner, hf, lane, whom):
        return [
            pltpu.make_async_remote_copy(
                src_ref=s,
                dst_ref=d,
                send_sem=wsend.at[lane, hf, i],
                recv_sem=wrecv.at[lane, hf, i],
                device_id=whom,
                device_id_type=MESH,
            )
            for i, (s, d) in enumerate(
                zip(src_refs, weight_parts(owner, hf), strict=True)
            )
        ]

    def own_parts(hf):
        return (
            gu_own.at[:, pl.ds(hf * half, half)],
            dn_own.at[pl.ds(hf * hhid, hhid)],
        )

    g_left, g_right, g_opp = lax.rem(g + 3, 4), lax.rem(g + 1, 4), lax.rem(g + 2, 4)
    weight_sends = []
    for turn in range(2):
        for lane, whom in ((0, right), (1, left)):
            hf = turn if lane == 0 else 1 - turn
            weight_sends += weight_copy(own_parts(hf), g, hf, lane, whom)
    for copy in weight_sends:
        copy.start()

    def slot_rows(h, q, ry, count=1):
        return xy.at[pl.ds(pl.multiple_of(((h * 4 + q) * ny + ry) * PAIR, PAIR), count * PAIR)]

    def near_copy(h, ry):
        sign = 1 - 2 * lax.rem(h + pz, 2)
        zt = lax.rem(z + sign * h + nz, nz)
        yt = lax.rem(y + ry, ny)
        to = yt * nh + lax.div(zt, 2)
        return pltpu.make_async_remote_copy(
            src_ref=pack.at[pl.ds(pl.multiple_of(to * PAIR, PAIR), PAIR)],
            dst_ref=slot_rows(h, 0, ry),
            send_sem=dsend,
            recv_sem=near_sem.at[h * ny + ry],
            device_id=device(yt, zt),
            device_id_type=MESH,
        )

    mine = pltpu.make_async_copy(
        pack.at[pl.ds(pl.multiple_of(lax.div(ei, 4) * PAIR, PAIR), PAIR)],
        slot_rows(0, 0, 0),
        near_sem.at[0],
    )
    mine.start()
    for h in range(min(nh, 3)):
        for ry in range(ny):
            if h or ry:
                near_copy(h, ry).start()

    def hand_on(h, q, ry, whom, to_q, send_sem, recv_sem):
        return pltpu.make_async_remote_copy(
            src_ref=slot_rows(h, q, ry),
            dst_ref=slot_rows(h, to_q, ry),
            send_sem=send_sem,
            recv_sem=recv_sem,
            device_id=whom,
            device_id_type=MESH,
        )

    def arrived(ref, sem):
        pltpu.make_async_copy(ref, ref, sem).wait()

    def pass_near(h, ry):
        arrived(slot_rows(h, 0, ry), near_sem.at[h * ny + ry])
        hand_on(h, 0, ry, mate, 1, psend, pair_sem.at[h * ny + ry]).start()
        hand_on(h, 0, ry, sib, 2, ssend, sib_sem.at[h, 0]).start()

    def pass_pair(h, ry):
        arrived(slot_rows(h, 1, ry), pair_sem.at[h * ny + ry])
        hand_on(h, 1, ry, sib, 3, ssend, sib_sem.at[h, 1]).start()

    def pass_weights(lane, hf, owner, whom):
        for i, ref in enumerate(weight_parts(owner, hf)):
            arrived(ref, wrecv.at[lane, hf, i])
        copies = weight_copy(weight_parts(owner, hf), owner, hf, 2, whom)
        for copy in copies:
            copy.start()
        return copies

    last = nh - 1
    for h in range(nh):
        for ry in range(ny):
            pass_near(h, ry)
        if 3 <= h + 2 < nh:
            for ry in range(ny):
                near_copy(h + 2, ry).start()
        if h:
            for ry in range(ny):
                pass_pair(h - 1, ry)
        if h == min(2, last):
            weight_sends += pass_weights(0, 0, g_left, right)
            weight_sends += pass_weights(1, 1, g_right, left)
    for h in range(last):
        for q in range(2):
            arrived(slot_rows(h, 2 + q, 0, ny), sib_sem.at[h, q])
    for copy in own_copies:
        copy.wait()
    for lane, hf, owner in (
        (0, 1, g_left),
        (1, 0, g_right),
        (2, 0, g_opp),
        (2, 1, g_opp),
    ):
        for i, ref in enumerate(weight_parts(owner, hf)):
            arrived(ref, wrecv.at[lane, hf, i])

    def z_copy(h):
        return pltpu.make_async_remote_copy(
            src_ref=zbuf.at[pl.ds(pl.multiple_of(h * batch + batch // 2, PAIR), batch // 2)],
            dst_ref=zrecv.at[pl.ds(pl.multiple_of(h * (batch // 2), PAIR), batch // 2)],
            send_sem=zsend.at[h],
            recv_sem=zwait.at[h],
            device_id=sib,
            device_id_type=MESH,
        )

    def rows_of(h):
        return pl.ds(pl.multiple_of(h * batch, batch), batch)

    def activations(h):
        rows = rows_of(h)
        pre = jnp.zeros((batch, hid), jnp.float32)
        up = jnp.zeros((batch, hid), jnp.float32)
        err = jnp.zeros((batch, hid), jnp.float32)
        for at in range(0, feat, kc):
            block = xy[rows, at : at + kc]
            pre += dot(block, wgu[0, at : at + kc])
            up += dot(block, wgu[1, at : at + kc])
            err += lax.dot_general(
                block,
                wd[:, at : at + kc],
                (((1,), (1,)), ((), ())),
                preferred_element_type=jnp.float32,
            )
        pre = pre.reshape(batch // PAIR, PAIR, hid)[:, :CAP]
        up = up.reshape(batch // PAIR, PAIR, hid)[:, :CAP]
        err = err.reshape(batch // PAIR, PAIR, hid)[:, CAP:]
        sig = jax.nn.sigmoid(pre)
        active = pre * sig * up
        d_gate = err * up * sig * (1.0 + pre * (1.0 - sig))
        d_up = err * pre * sig
        none = jnp.zeros_like(active)
        spread = jnp.concatenate(
            [
                jnp.concatenate([d_gate, d_up, none], axis=2),
                jnp.concatenate([none, none, active], axis=2),
            ],
            axis=1,
        )
        spread = spread.reshape(batch, 3 * hid).astype(jnp.bfloat16)
        return spread, active.reshape(batch // 2, hid).astype(jnp.bfloat16)

    def weight_grad(h, owner, spread):
        at = pl.ds(pl.multiple_of(owner * part, 128), part)
        return gacc[at] + lax.dot_general(
            xy[rows_of(h), at],
            spread,
            (((0,), (0,)), ((), ())),
            preferred_element_type=jnp.float32,
        )

    def project(h, act):
        kz = 256 if lanes % 256 == 0 else 128
        for at in range(0, lanes, kz):
            low = dot(act, wd[:, at : at + kz])
            top = dot(act, wd[:, lanes + at : lanes + at + kz])
            both = jnp.concatenate(
                [
                    low.reshape(batch // PAIR, CAP, kz),
                    top.reshape(batch // PAIR, CAP, kz),
                ],
                axis=1,
            )
            zbuf[rows_of(h), at : at + kz] = both.reshape(batch, kz).astype(jnp.bfloat16)
        z_copy(h).start()

    def pass_some(h, piece):
        for ry in range(ny):
            at = min(ry, 2 * last - 1)

            @pl.when(h * 2 + piece == at)
            def _(ry=ry):
                pass_pair(last, ry)

    def step(h, carry):
        spread, act = activations(h)
        pass_some(h, 0)
        for owner in range(4):
            gacc[owner * part : (owner + 1) * part] = weight_grad(h, owner, spread)
        project(h, act)
        pass_some(h, 1)
        return carry

    lax.fori_loop(0, last, step, 0)
    for q in range(2):
        arrived(slot_rows(last, 2 + q, 0, ny), sib_sem.at[last, q])

    def own_rows(owner):
        return pl.ds(pl.multiple_of(owner * part, 128), part)

    def grad_copy(k, src, dst, whom):
        return pltpu.make_async_remote_copy(
            src_ref=src,
            dst_ref=dst,
            send_sem=rsend.at[k],
            recv_sem=rwait.at[k],
            device_id=whom,
            device_id_type=MESH,
        )

    def piece_of(n):
        return pl.ds(n * half, half)

    grad_sends = [
        grad_copy(0, gs.at[0, 0, piece_of(0)], part_l.at[piece_of(0)], right),
        grad_copy(1, gs.at[0, 0, piece_of(1)], part_l.at[piece_of(1)], right),
        grad_copy(2, gs.at[0, 1, piece_of(0)], part_r.at[piece_of(0)], left),
        grad_copy(3, gs.at[0, 1, piece_of(1)], part_r.at[piece_of(1)], left),
        grad_copy(4, gs.at[1, 1], from_l.at[1], right),
        grad_copy(5, gs.at[2, 0], from_r.at[0], left),
        grad_copy(6, gs.at[1, 0, piece_of(0)], from_l.at[0, piece_of(0)], right),
        grad_copy(7, gs.at[1, 0, piece_of(1)], from_l.at[0, piece_of(1)], right),
        grad_copy(8, gs.at[2, 1, piece_of(0)], from_r.at[1, piece_of(0)], left),
        grad_copy(9, gs.at[2, 1, piece_of(1)], from_r.at[1, piece_of(1)], left),
    ]
    spread, act = activations(last)
    wide = gacc.shape[1] // 2
    for slot, owner, sent in ((0, g_opp, ((0, 0), (2, 1))), (1, g_right, ((4, 1),)), (2, g_left, ((5, 0),))):
        full = weight_grad(last, owner, spread)
        for k, hf in sent:
            gs[slot, hf] = full[:, hf * wide : (hf + 1) * wide].astype(jnp.bfloat16)
            grad_sends[k].start()
            if not slot:
                grad_sends[k + 1].start()
        if slot:
            hf = 1 - sent[0][1]
            gacc[own_rows(owner), hf * wide : (hf + 1) * wide] = full[
                :, hf * wide : (hf + 1) * wide
            ]

    def o_copy(h, q, ry):
        ys = lax.rem(y - ry + ny, ny)
        if q == 0:
            zs = lax.rem(z + (2 * pz - 1) * h + nz, nz)
        else:
            zs = lax.rem(z + (1 - 2 * pz) * (1 + h) + nz, nz)
        return pltpu.make_async_remote_copy(
            src_ref=sbuf.at[pl.ds(pl.multiple_of(((h * 2 + q) * ny + ry) * PAIR, PAIR), PAIR)],
            dst_ref=orecv.at[pl.ds(pl.multiple_of((pz * experts + lax.div(ei, 4)) * PAIR, PAIR), PAIR)],
            send_sem=osend,
            recv_sem=owait,
            device_id=device(ys, zs),
            device_id_type=MESH,
        )

    here = pl.ds(
        pl.multiple_of((pz * experts + lax.div(ei, 4)) * PAIR, PAIR), PAIR
    )

    def send_back(h):
        z_copy(h).wait_recv()
        a, b = h * batch, h * (batch // 2)
        total = zbuf[a : a + batch // 2].astype(jnp.float32) + zrecv[
            b : b + batch // 2
        ].astype(jnp.float32)
        sbuf[b : b + batch // 2] = total.astype(jnp.bfloat16)
        for q in range(2):
            for ry in range(ny):
                if h or q or ry:
                    o_copy(h, q, ry).start()
                else:
                    pltpu.make_async_copy(
                        sbuf.at[pl.ds(0, PAIR)], orecv.at[here], owait
                    ).start()

    project(last, act)
    for h in range(last):
        send_back(h)
    gacc[own_rows(g)] = weight_grad(last, g, spread)
    send_back(last)

    for n in range(2):
        for k, came, slot, hf, owner in (
            (0, part_l, 1, 0, g_right),
            (2, part_r, 2, 1, g_left),
        ):
            arrived(came.at[piece_of(n)], rwait.at[k + n])
            rows = pl.ds(pl.multiple_of(owner * part + n * half, 64), half)
            gs[slot, hf, n * half : (n + 1) * half] = (
                gacc[rows, hf * wide : (hf + 1) * wide]
                + came[n * half : (n + 1) * half].astype(jnp.float32)
            ).astype(jnp.bfloat16)
            grad_sends[6 + k + n].start()

    for k, came, hf in ((5, from_r, 0), (4, from_l, 1)):
        arrived(came.at[hf], rwait.at[k])
        cols = slice(hf * wide, (hf + 1) * wide)
        gacc[own_rows(g), cols] = gacc[own_rows(g), cols] + came[hf].astype(jnp.float32)

    arrived(orecv, owait)
    for side in range(2):
        done = jnp.zeros((rows_t, lanes), jnp.float32)
        for which in range(2):
            part_o = orecv[which * experts * PAIR : (which + 1) * experts * PAIR]
            part_o = part_o.astype(jnp.float32).reshape(experts, PAIR, lanes)
            part_o = part_o[:, side * CAP : (side + 1) * CAP].reshape(slots, lanes)
            part_o = part_o.astype(jnp.bfloat16)
            done += dot(comb[0], part_o) + dot(comb[1], part_o)
        out[:, side * lanes : (side + 1) * lanes] = done.astype(jnp.bfloat16)

    totals = []
    for k, came, hf in ((6, from_l, 0), (8, from_r, 1)):
        for n in range(2):
            arrived(came.at[hf, piece_of(n)], rwait.at[k + n])
        cols = slice(hf * wide, (hf + 1) * wide)
        totals.append(gacc[own_rows(g), cols] + came[hf].astype(jnp.float32))
    gpair[0] = totals[0][:, :hid]
    gpair[1, :, : hid // 2] = totals[0][:, hid:]
    gpair[1, :, hid // 2 :] = totals[1][:, : hid // 2]
    gdown[...] = totals[1][:, hid // 2 :].T

    for copy in weight_sends + grad_sends:
        copy.wait_send()
    for h in range(nh):
        z_copy(h).wait_send()
    count = nh * ny
    arrived(xy.at[pl.ds(0, (count - 1) * PAIR)], dsend)
    arrived(xy.at[pl.ds(0, count * PAIR)], psend)
    arrived(xy.at[pl.ds(0, 2 * count * PAIR)], ssend)
    arrived(sbuf.at[pl.ds(0, (2 * count - 1) * PAIR)], osend)


def experts_step(tokens, cotangent, expert_ids, gate_weights, pair_own, down_own):
    shards = lax.axis_size("expert")
    ny, nz = NY, shards // (2 * NY)
    nh = nz // 2
    experts = shards // SPLIT
    rows, feat = tokens.shape
    hid = down_own.shape[0]
    part, lanes, wide = feat // 4, feat // 2, 3 * hid // 2
    slots = experts * CAP
    batch = 4 * ny * PAIR
    vmem = pl.BlockSpec(memory_space=pltpu.VMEM)
    hbm = pl.BlockSpec(memory_space=pltpu.HBM)
    bf, f32 = jnp.bfloat16, jnp.float32
    dma = pltpu.SemaphoreType.DMA
    return pl.pallas_call(
        functools.partial(moe_kernel, ny, nz),
        out_shape=(
            jax.ShapeDtypeStruct((rows, feat), bf),
            jax.ShapeDtypeStruct((2, part, hid), f32),
            jax.ShapeDtypeStruct((hid, part), f32),
        ),
        in_specs=[hbm] * 6,
        out_specs=(vmem, vmem, vmem),
        scratch_shapes=[
            pltpu.VMEM((rows, feat), bf),
            pltpu.VMEM((rows, feat), bf),
            pltpu.VMEM((TOP, rows), jnp.int32),
            pltpu.VMEM((TOP, rows), f32),
            pltpu.VMEM((experts * PAIR, feat), bf),
            pltpu.VMEM((2, rows, slots), bf),
            pltpu.VMEM((nh * batch, feat), bf),
            pltpu.VMEM((2, feat, hid), bf),
            pltpu.VMEM((hid, feat), bf),
            pltpu.VMEM((feat, 3 * hid), f32),
            pltpu.VMEM((3, 2, part, wide), bf),
            pltpu.VMEM((part, wide), bf),
            pltpu.VMEM((part, wide), bf),
            pltpu.VMEM((2, part, wide), bf),
            pltpu.VMEM((2, part, wide), bf),
            pltpu.VMEM((nh * batch, lanes), bf),
            pltpu.VMEM((nh * batch // 2, lanes), bf),
            pltpu.VMEM((nh * batch // 2, lanes), bf),
            pltpu.VMEM((2 * experts * PAIR, lanes), bf),
            dma((2,)),
            dma((3, 2, 2)),
            dma((3, 2, 2)),
            dma,
            dma,
            dma,
            dma((nh * ny,)),
            dma((nh * ny,)),
            dma((nh, 2)),
            dma((nh,)),
            dma((nh,)),
            dma,
            dma,
            dma((10,)),
            dma((10,)),
            dma((4,)),
        ],
        compiler_params=pltpu.CompilerParams(
            collective_id=0,
            has_side_effects=True,
            vmem_limit_bytes=46 * 1024 * 1024,
        ),
        cost_estimate=pl.CostEstimate(
            flops=8_000_000_000, bytes_accessed=10_000_000, transcendentals=200_000
        ),
    )(
        *(
            pltpu.with_memory_space_constraint(a, pltpu.HBM)
            for a in (
                tokens,
                cotangent,
                expert_ids.T,
                gate_weights.T,
                pair_own,
                down_own,
            )
        )
    )


def update_kernel(*refs):
    ins, outs, scratch, sem = refs[:9], refs[9:16], refs[16:22], refs[22]
    copies = [pltpu.make_async_copy(ins[8], outs[6], sem.at[0])]
    copies[0].start()
    for which in range(2):
        weight, gradient, first, second = ins[which * 4 : which * 4 + 4]
        kept, to = scratch[which * 3 : which * 3 + 3], outs[which * 3 : which * 3 + 3]
        rows = weight.shape[0]
        count = 8 if which == 0 else 4
        size = rows // count
        for at in range(0, rows, size):
            piece = slice(at, at + size)
            made = adamw_update(
                weight[piece], gradient[piece], first[piece], second[piece]
            )
            for value, keep, end in zip(made, kept, to, strict=True):
                keep[piece] = value
                copies.append(
                    pltpu.make_async_copy(
                        keep.at[pl.ds(at, size)],
                        end.at[pl.ds(at, size)],
                        sem.at[len(copies)],
                    )
                )
                copies[-1].start()
    for copy in copies:
        copy.wait()


def update(pair, down, layer_out):
    vmem = pl.BlockSpec(memory_space=pltpu.VMEM)
    hbm = pl.BlockSpec(memory_space=pltpu.HBM)
    kinds = []
    for group in (pair, down):
        for dtype in (jnp.bfloat16, jnp.float32, jnp.float32):
            kinds.append((group[0].shape, dtype))
    return pl.pallas_call(
        update_kernel,
        out_shape=tuple(
            jax.ShapeDtypeStruct(*kind)
            for kind in (*kinds, (layer_out.shape, layer_out.dtype))
        ),
        in_specs=[vmem] * 9,
        out_specs=(hbm,) * 7,
        scratch_shapes=[pltpu.VMEM(*kind) for kind in kinds]
        + [pltpu.SemaphoreType.DMA((37,))],
        compiler_params=pltpu.CompilerParams(vmem_limit_bytes=32 * 1024 * 1024),
        cost_estimate=pl.CostEstimate(
            flops=15_000_000, bytes_accessed=12_000_000, transcendentals=1_000_000
        ),
    )(*pair, *down, layer_out)


def body(
    tokens,
    cotangent,
    expert_ids,
    gate_weights,
    gate_up,
    down_proj,
    gate_up_first,
    gate_up_second,
    down_first,
    down_second,
):
    layer_out, own_pair, own_down = experts_step(
        tokens, cotangent, expert_ids, gate_weights, gate_up[0], down_proj[0]
    )

    def flat(a):
        return a.reshape(-1, a.shape[-1])

    pair = [flat(a) for a in (gate_up, own_pair, gate_up_first, gate_up_second)]
    down = [flat(a) for a in (down_proj, own_down, down_first, down_second)]
    made = update(pair, down, layer_out)
    pair_new = [a.reshape(gate_up.shape) for a in made[:3]]
    down_new = [a.reshape(down_proj.shape) for a in made[3:6]]
    return (
        made[6],
        pair_new[0],
        down_new[0],
        pair_new[1],
        pair_new[2],
        down_new[1],
        down_new[2],
    )


def solution(mesh):
    return jax.shard_map(
        body,
        mesh=mesh,
        in_specs=(
            P(("dp", "expert"), None),
            P(("dp", "expert"), None),
            P(("dp", "expert"), None),
            P(("dp", "expert"), None),
            P("expert", None, "dp", None),
            P("expert", None, "dp"),
            P("expert", None, "dp", None),
            P("expert", None, "dp", None),
            P("expert", None, "dp"),
            P("expert", None, "dp"),
        ),
        out_specs=(
            P(("dp", "expert"), None),
            P("expert", None, "dp", None),
            P("expert", None, "dp"),
            P("expert", None, "dp", None),
            P("expert", None, "dp", None),
            P("expert", None, "dp"),
            P("expert", None, "dp"),
        ),
        check_vma=False,
    )
```
